256 devices in a mesh: dp: 64 (over x, z, y_lo), head: 4 (over y_hi, core).
Axes of the slice: x: 4, y: 4 (y_hi: 2, y_lo: 2; y = y_hi * 2 + y_lo), z: 8, core: 2. Of those that a mesh axis runs over, the one named last changes fastest.
Arguments:
- vision_tokens: bfloat16 [512, 256, 1536], P('dp', 'head'), may hold values from -6 to 6
- memory_projector: bfloat16 [1536, 2, 1536], P(None, None, 'head'), may hold values from -0.15625 to 0.15625
- query_vectors: bfloat16 [16, 96], P('head'), may hold values from -4 to 4
- final_projector: bfloat16 [1536, 1536], P('head'), may hold values from -0.89304314 to 0.89304314
- caption_vectors: bfloat16 [512, 1536], P('dp'), may hold values from -40 to 40
- logit_multiplier: float32 [], replicated, may hold values from 8 to 16
- logit_shift: float32 [], replicated, may hold values from -4 to -2
Outputs:
- image_grad: float32 [512, 1536], P(('dp', 'head'))
- text_grad: float32 [512, 1536], P(('dp', 'head'))
The draws below stay inside these ranges and needn't reach their ends.
All inputs are finite; a program needn't handle non-finite values.
Results may differ from the reference program's by a relative error of at most 0.0055.
Values may be sent and summed in bfloat16 or wider, within the bound.
No kernel may reach another device: no remote copies, remote signals or barrier semaphores. Data moves between devices by JAX's collectives and lax.ppermute only.
A program may use at most 64 MiB of HBM per device.

```python
import math
import jax
import jax.numpy as jnp
from jax import lax

WIDTH = 1536
HEADS = 16
PATCHES = 256
HEAD_DIM = 96
PAIRS_DEV = 8
PAIRS = 512
N_DP = 64


def column_scales(scale_key):
    return jnp.exp(jax.random.uniform(scale_key, (WIDTH,), jnp.float32, 0.0, math.log(10.0)))


def draw_final_projector(key, part):
    key = jax.random.fold_in(key, 7)
    scale_key, entry_key = jax.random.split(key)
    column_scale = column_scales(scale_key)
    entries = jnp.clip(jax.random.normal(entry_key, (WIDTH, WIDTH), jnp.float32), -3.5, 3.5)
    return (entries * column_scale / math.sqrt(WIDTH)).astype(jnp.bfloat16)


def draw_caption_vectors(key, part):
    key = jax.random.fold_in(key, 11)
    scale_key, entry_key = jax.random.split(key, 2)
    column_scale = column_scales(scale_key)
    entries = jnp.clip(jax.random.normal(entry_key, (PAIRS, WIDTH), jnp.float32), -3.5, 3.5)
    return jnp.clip(entries * column_scale, -40.0, 40.0).astype(jnp.bfloat16)


def shard_levels(stream_key, shape, pieces, least, largest):
    def one(axis_at, parts):
        heights = jax.random.uniform(jax.random.fold_in(jax.random.fold_in(stream_key, 6), axis_at), (parts,), jnp.float32, least / len(pieces), largest / len(pieces))
        return jnp.repeat(jnp.exp(heights), shape[axis_at] // parts).reshape((-1,) + (1,) * (len(shape) - axis_at - 1))

    level = one(*pieces[0])
    for cut in pieces[1:]:
        level = level * one(*cut)
    return level


def centred(stream_key, dims, width, reach, cuts=(), kind=jnp.bfloat16):
    factor_of = shard_levels(stream_key, dims, cuts, -0.22, 0.18) if cuts else 1.0
    values = jax.random.normal(stream_key, dims, jnp.float32) * width * factor_of
    return jnp.minimum(jnp.maximum(values, -reach), reach).astype(kind)


def setup_inputs(seed: int = 0) -> dict:
    arg_keys = jax.random.split(jax.random.key(seed), 8)
    vision_tokens = centred(arg_keys[0], (PAIRS, PATCHES, WIDTH), 1.0, 6.0, ((0, 64), (1, 4)))
    memory_projector = centred(arg_keys[1], (WIDTH, 2, WIDTH), WIDTH ** -0.5, 0.15625, ((2, 4),))
    query_vectors = centred(arg_keys[2], (HEADS, HEAD_DIM), 1.0, 4.0, ((0, 4),))
    final_projector = draw_final_projector(jax.random.fold_in(arg_keys[7], 71), 0)
    caption_vectors = draw_caption_vectors(jax.random.fold_in(arg_keys[7], 71), 0)
    logit_multiplier = jnp.clip(jax.random.uniform(arg_keys[5], (), jnp.float32, 8.0, 16.0), 8.0, 16.0)
    logit_shift = jnp.clip(jax.random.uniform(arg_keys[6], (), jnp.float32, -4.0, -2.0), -4.0, -2.0)
    return dict(vision_tokens=vision_tokens, memory_projector=memory_projector, query_vectors=query_vectors, final_projector=final_projector, caption_vectors=caption_vectors, logit_multiplier=logit_multiplier, logit_shift=logit_shift)


def unit_rows(values):
    widened = values.astype(jnp.float32)
    return (widened * lax.rsqrt(lax.optimization_barrier(jnp.sum(widened * widened, -1, keepdims=True)) + 1e-06)).astype(jnp.bfloat16)

def pool_block(block_tokens, memory_projector, query_vectors):
    image_count = block_tokens.shape[0]
    flattened = block_tokens.reshape(image_count * PATCHES, WIDTH)
    projection = memory_projector.reshape(WIDTH, 2 * WIDTH)
    keys_values = jnp.dot(flattened, projection, preferred_element_type=jnp.float32).astype(jnp.bfloat16)
    keys_values = keys_values.reshape(image_count, PATCHES, 2, HEADS, HEAD_DIM)
    key_rows = keys_values[:, :, 0].astype(jnp.float32)
    value_rows = keys_values[:, :, 1].astype(jnp.float32)
    scores = jnp.einsum('bphe,he->bhp', key_rows, query_vectors.astype(jnp.float32)) / math.sqrt(HEAD_DIM)
    raised = jnp.exp(scores)
    weights = (raised / lax.optimization_barrier(jnp.sum(raised, -1, keepdims=True))).astype(jnp.bfloat16)
    pooled = jnp.einsum('bhp,bphe->bhe', weights.astype(jnp.float32), value_rows).astype(jnp.bfloat16)
    return pooled.reshape(image_count, WIDTH)

def reference(vision_tokens, memory_projector, query_vectors, final_projector, caption_vectors, logit_multiplier, logit_shift):
    blocks = vision_tokens.reshape(N_DP, PAIRS_DEV, PATCHES, WIDTH)
    pooled = lax.map(lambda block_tokens: pool_block(block_tokens, memory_projector, query_vectors), blocks)
    pooled = pooled.reshape(PAIRS, WIDTH)
    embedding = jnp.dot(pooled, final_projector, preferred_element_type=jnp.float32)
    picture_unitlength = unit_rows(embedding)
    caption_unitlength = unit_rows(caption_vectors)
    match_scores = logit_multiplier * jnp.dot(picture_unitlength, caption_unitlength.T, preferred_element_type=jnp.float32) + logit_shift
    row_ids = jnp.arange(PAIRS, dtype=jnp.int32)
    matched_scores = (row_ids[:, None] == row_ids[None, :]).astype(jnp.float32)
    objective_factor = (logit_multiplier * (jax.nn.sigmoid(match_scores) - matched_scores)).astype(jnp.bfloat16)
    image_grad = jnp.dot(objective_factor, caption_unitlength, preferred_element_type=jnp.float32)
    text_grad = jnp.dot(objective_factor.T, picture_unitlength, preferred_element_type=jnp.float32)
    return (image_grad, text_grad)
```

```python
import math

import jax
import jax.numpy as jnp
from jax import lax
from jax.sharding import PartitionSpec as P

F32 = jnp.float32
BF16 = jnp.bfloat16


def unit_rows(values):
    widened = values.astype(F32)
    return (widened * lax.rsqrt(jnp.sum(widened * widened, -1, keepdims=True) + 1e-06)).astype(BF16)


def split_two(values):
    high = values.astype(BF16)
    return high, (values - high.astype(F32)).astype(BF16)


def split_three(values):
    high = values.astype(BF16)
    rest = values - high.astype(F32)
    middle = rest.astype(BF16)
    return high, middle, (rest - middle.astype(F32)).astype(BF16)


def peers(piece_of):
    parts = [piece_of(0)]
    for step in (1, 2, 3):
        parts.append(lax.ppermute(piece_of(step), "head", [(i, i ^ step) for i in range(4)]))
    return parts


def per_device(tokens, projector, queries, final, captions, multiplier, shift):
    images, tokens_here, width = tokens.shape
    heads, head_size = queries.shape
    n_dp = lax.axis_size("dp")
    share = images // 4
    dp = lax.axis_index("dp")
    head = lax.axis_index("head")

    text_unit = unit_rows(lax.dynamic_slice_in_dim(captions, head * share, share, 0))
    texts = lax.all_to_all(
        jnp.broadcast_to(text_unit[None], (n_dp, share, width)), "dp", 0, 0, tiled=False
    ).reshape(n_dp * share, width)

    key_part = projector[:, 0, :].reshape(width, heads, head_size)
    key_query = jnp.einsum("ihe,he->hi", key_part, queries, preferred_element_type=F32)
    key_query = key_query / math.sqrt(head_size)
    high, low = split_two(key_query)
    packed = jnp.concatenate([high, low], 0)
    gathered = peers(lambda s: packed)
    high = jnp.concatenate([part[:heads] for part in gathered], 0)
    low = jnp.concatenate([part[heads:] for part in gathered], 0)
    both = jnp.concatenate([high, low], 0)
    rows = tokens.reshape(images * tokens_here, width)
    raw = lax.dot_general(rows, both, (((1,), (1,)), ((), ())), preferred_element_type=F32)
    scores = (raw[:, : 4 * heads] + raw[:, 4 * heads :]).reshape(images, tokens_here, 4 * heads)
    top = jnp.max(scores, 1, keepdims=True)
    raised = jnp.exp(scores - top)
    total = jnp.sum(raised, 1, keepdims=True)
    weights = (raised / total).astype(BF16)
    mixed = jnp.einsum("nph,npi->hni", weights, tokens, preferred_element_type=F32).astype(BF16)
    log_total = (top + jnp.log(total))[:, 0, :].T
    pieces = jnp.stack(split_three(log_total), -1)
    message = jnp.concatenate(
        [mixed, jnp.pad(pieces, ((0, 0), (0, 0), (0, 125)))], -1
    ).reshape(4, heads * images, width + 128)
    parts = peers(lambda s: message[s])
    logs = [jnp.sum(part[:, width : width + 3].astype(F32), -1, keepdims=True) for part in parts]
    peak = jnp.maximum(jnp.maximum(logs[0], logs[1]), jnp.maximum(logs[2], logs[3]))
    shares = [jnp.exp(entry - peak) for entry in logs]
    whole = shares[0] + shares[1] + shares[2] + shares[3]
    token_mix = sum(s / whole * part[:, :width].astype(F32) for s, part in zip(shares, parts))
    token_mix = token_mix.astype(BF16).reshape(heads, images, width)
    value_part = projector[:, 1, :].reshape(width, heads, head_size)
    pooled = jnp.einsum("hni,ihe->nhe", token_mix, value_part, preferred_element_type=F32)
    pooled = pooled.astype(BF16).reshape(images, heads * head_size)
    partial = jnp.dot(pooled, final, preferred_element_type=F32)
    embeds = peers(lambda s: partial)
    image_unit = unit_rows((embeds[0] + embeds[1]) + (embeds[2] + embeds[3]))

    similarity = lax.dot_general(
        image_unit, texts, (((1,), (1,)), ((), ())), preferred_element_type=F32
    )
    logits = multiplier * similarity + shift
    image_ids = dp * images + jnp.arange(images, dtype=jnp.int32)
    column = jnp.arange(n_dp * share, dtype=jnp.int32)
    text_ids = column // share * images + head * share + column % share
    matched = (image_ids[:, None] == text_ids[None, :]).astype(F32)
    coefficient = (multiplier * (jax.nn.sigmoid(logits) - matched)).astype(BF16)

    text_part = lax.dot_general(
        coefficient, image_unit, (((0,), (0,)), ((), ())), preferred_element_type=F32
    )
    text_part = text_part.astype(BF16).reshape(n_dp, share, width)
    text_grad = jnp.sum(
        lax.all_to_all(text_part, "dp", 0, 0, tiled=False).astype(F32), 0
    )
    image_part = jnp.dot(coefficient, texts, preferred_element_type=F32)
    grads = peers(
        lambda s: lax.dynamic_slice_in_dim(image_part, (head ^ s) * share, share, 0)
    )
    image_grad = (grads[0] + grads[1]) + (grads[2] + grads[3])
    return image_grad, text_grad


def solution(mesh):
    in_specs = (
        P("dp", "head", None),
        P(None, None, "head"),
        P("head", None),
        P("head", None),
        P("dp", None),
        P(),
        P(),
    )
    out_specs = (P(("dp", "head"), None), P(("dp", "head"), None))
    return jax.shard_map(
        per_device, mesh=mesh, in_specs=in_specs, out_specs=out_specs, check_vma=False
    )
```

```python
import math

import jax
import jax.numpy as jnp
from jax import lax
from jax.experimental import pallas as pl
from jax.experimental.pallas import tpu as pltpu
from jax.sharding import PartitionSpec as P

F32 = jnp.float32
BF16 = jnp.bfloat16
NT = (((1,), (1,)), ((), ()))
TN = (((0,), (0,)), ((), ()))
VMEM = pl.BlockSpec(memory_space=pltpu.VMEM)
ANY = pl.BlockSpec(memory_space=pl.ANY)
SMEM = pl.BlockSpec(memory_space=pltpu.SMEM)


def call(kernel, outs, specs, flops, moved):
    return pl.pallas_call(
        kernel,
        grid=(1,),
        out_shape=outs,
        in_specs=specs,
        out_specs=jax.tree.map(lambda _: VMEM, outs),
        compiler_params=pltpu.CompilerParams(vmem_limit_bytes=10 << 20),
        cost_estimate=pl.CostEstimate(flops=flops, bytes_accessed=moved, transcendentals=0),
    )


def unit_rows(values):
    widened = values.astype(F32)
    return (widened * lax.rsqrt(jnp.sum(widened * widened, -1, keepdims=True) + 1e-06)).astype(BF16)


def peers(pieces):
    return [pieces[0]] + [
        lax.ppermute(pieces[s], "head", [(i, i ^ s) for i in range(4)]) for s in (1, 2, 3)
    ]


def key_query_kernel(spread_ref, key_ref, out_ref, *, scale):
    out_ref[...] = (
        lax.dot_general(spread_ref[...], key_ref[...], NT, preferred_element_type=F32) * scale
    )


def mix_kernel(tokens_ref, q0, q1, q2, q3, m0, m1, m2, m3, *, images):
    count, here, width = tokens_ref.shape
    rows = tokens_ref[...].reshape(count * here, width)
    heads = q0.shape[0]
    spread = jnp.concatenate(
        [
            jnp.broadcast_to(ref[h : h + 1, :], (images, width))
            for ref in (q0, q1, q2, q3)
            for h in range(heads)
        ],
        0,
    )
    columns = spread.shape[0]
    high = spread.astype(BF16)
    low = (spread - high.astype(F32)).astype(BF16)
    raw = lax.dot_general(rows, jnp.concatenate([high, low], 0), NT, preferred_element_type=F32)
    scores = raw[:, :columns] + raw[:, columns:]
    row_image = lax.broadcasted_iota(jnp.int32, scores.shape, 0) // here
    column_image = lax.broadcasted_iota(jnp.int32, scores.shape, 1) % images
    mine = row_image == column_image
    top = jnp.max(jnp.where(mine, scores, -jnp.inf), 0, keepdims=True)
    raised = jnp.exp(jnp.where(mine, scores - top, -jnp.inf))
    total = jnp.sum(raised, 0, keepdims=True)
    weights = (raised / total).astype(BF16)
    mixed = lax.dot_general(weights, rows, TN, preferred_element_type=F32).astype(BF16)
    log_total = jnp.broadcast_to(top + jnp.log(total), (columns, columns))
    down = lax.broadcasted_iota(jnp.int32, (columns, columns), 0)
    across = lax.broadcasted_iota(jnp.int32, (columns, columns), 1)
    upright = jnp.sum(jnp.where(down == across, log_total, 0.0), 1, keepdims=True)
    high = upright.astype(BF16).astype(F32)
    middle = (upright - high).astype(BF16).astype(F32)
    low = upright - high - middle
    lane = lax.broadcasted_iota(jnp.int32, (columns, 128), 1)
    pieces = jnp.where(lane == 0, high, jnp.where(lane == 1, middle, jnp.where(lane == 2, low, 0.0)))
    pieces = pieces.astype(BF16)
    step = columns // 4
    for s, ref in enumerate((m0, m1, m2, m3)):
        ref[:, :width] = mixed[s * step : (s + 1) * step]
        ref[:, width:] = pieces[s * step : (s + 1) * step]


def embed_kernel(m0, m1, m2, m3, value_ref, final_ref, out_ref, *, heads):
    width = value_ref.shape[0]
    parts = (m0, m1, m2, m3)
    logs = [jnp.sum(ref[:, width:].astype(F32), -1, keepdims=True) for ref in parts]
    peak = jnp.maximum(jnp.maximum(logs[0], logs[1]), jnp.maximum(logs[2], logs[3]))
    shares = [jnp.exp(entry - peak) for entry in logs]
    whole = (shares[0] + shares[1]) + (shares[2] + shares[3])
    mixed = sum((s / whole) * ref[:, :width].astype(F32) for s, ref in zip(shares, parts))
    pooled = jnp.dot(mixed.astype(BF16), value_ref[...], preferred_element_type=F32)
    rows, columns = pooled.shape
    images = rows // heads
    row_head = lax.broadcasted_iota(jnp.int32, pooled.shape, 0) // images
    column_head = lax.broadcasted_iota(jnp.int32, pooled.shape, 1) // (columns // heads)
    kept = jnp.where(row_head == column_head, pooled, 0.0)
    pooled = sum(kept[h * images : (h + 1) * images] for h in range(heads))
    out_ref[...] = jnp.dot(pooled.astype(BF16), final_ref[...], preferred_element_type=F32)


def text_kernel(place_ref, captions_ref, order_ref, out_ref):
    core = place_ref[1] % 2
    unit = unit_rows(captions_ref[...]).astype(F32)
    first = jnp.concatenate([unit[0:2], unit[4:6]], 0)
    second = jnp.concatenate([unit[2:4], unit[6:8]], 0)
    chosen = jnp.where(core == 0, first, second).astype(BF16)
    out_ref[...] = jnp.broadcast_to(chosen[None], out_ref.shape)


def text_ids(shape, first_dp, images, head):
    column = lax.broadcasted_iota(jnp.int32, shape, 1)
    return (first_dp + column // 4) * images + column % 4 // 2 * 4 + head % 2 * 2 + column % 2


def unit_kernel(e0, e1, e2, e3, order1, order2, order3, unit_ref):
    embed = (e0[...] + e1[...]) + (e2[...] + e3[...])
    unit_ref[...] = unit_rows(embed)


def text_grad_kernel(place_ref, scalar_ref, u0, u1, u2, u3, text_ref, order_ref, part_ref, *, near):
    dp, head = place_ref[0], place_ref[1]
    multiplier, shift = scalar_ref[0], scalar_ref[1]
    images, width = u0.shape
    chunk = width // 4
    block = dp // near
    units = jnp.concatenate([ref[...].astype(F32) for ref in (u0, u1, u2, u3)], 0)
    logits = lax.dot_general(units.astype(BF16), text_ref[...], NT, preferred_element_type=F32)
    logits = logits * multiplier + shift
    row = lax.broadcasted_iota(jnp.int32, logits.shape, 0)
    image_id = ((block ^ (row // images)) * near + dp % near) * images + row % images
    text_id = text_ids(logits.shape, block * near, images, head)
    matched = jnp.where(image_id == text_id, 1.0, 0.0)
    coefficient = (multiplier * (jax.nn.sigmoid(logits) - matched)).astype(BF16)
    source = lax.broadcasted_iota(jnp.int32, (near * 4, near * 8), 0)
    target = lax.broadcasted_iota(jnp.int32, (near * 4, near * 8), 1)
    repeat = jnp.where(source == target // 8 * 4 + head // 2 * 2 + target % 8 // 4, 1.0, 0.0)
    wide = jnp.dot(coefficient, repeat.astype(BF16), preferred_element_type=F32)
    wide = jnp.concatenate([wide] * 4, 0)
    row_chunk = lax.broadcasted_iota(jnp.int32, wide.shape, 0) // (4 * images)
    column_chunk = lax.broadcasted_iota(jnp.int32, wide.shape, 1) % 4
    wide = jnp.where(row_chunk == column_chunk, wide, 0.0).astype(BF16)
    stacked = jnp.concatenate([units[:, c * chunk : (c + 1) * chunk] for c in range(4)], 0)
    part = lax.dot_general(wide, stacked.astype(BF16), TN, preferred_element_type=F32)
    part_ref[...] = part.reshape(part_ref.shape).astype(part_ref.dtype)


def image_grad_kernel(
    place_ref, scalar_ref, unit_ref, t0, t1, t2, t3, own_ref, other_ref, *, near
):
    dp, head = place_ref[0], place_ref[1]
    multiplier, shift = scalar_ref[0], scalar_ref[1]
    images, width = unit_ref.shape
    share = images // 4
    block = dp // near
    grads = jnp.zeros((images, width), F32)
    for s, ref in enumerate((t0, t1, t2, t3)):
        texts = ref[...]
        logits = lax.dot_general(unit_ref[...], texts, NT, preferred_element_type=F32)
        logits = logits * multiplier + shift
        image_id = dp * images + lax.broadcasted_iota(jnp.int32, logits.shape, 0)
        text_id = text_ids(logits.shape, (block ^ s) * near, images, head)
        matched = jnp.where(image_id == text_id, 1.0, 0.0)
        coefficient = (multiplier * (jax.nn.sigmoid(logits) - matched)).astype(BF16)
        grads = grads + jnp.dot(coefficient, texts, preferred_element_type=F32)
    for wanted, ref in ((head, own_ref), (head ^ 1, other_ref)):
        ref[...] = sum(
            jnp.where(wanted == k, grads[k * share : (k + 1) * share], 0.0) for k in range(4)
        )


def sum_kernel(part_ref, out_ref):
    share, width = out_ref.shape
    chunk = part_ref.shape[2]
    total = jnp.sum(part_ref[...].astype(F32), 0)
    for r in range(share):
        for c in range(4):
            out_ref[r : r + 1, c * chunk : (c + 1) * chunk] = total[r * 4 + c : r * 4 + c + 1]


def per_device(tokens, projector, queries, final, captions, multiplier, shift):
    images, here, width = tokens.shape
    heads, head_size = queries.shape
    n_dp = lax.axis_size("dp")
    near = n_dp // 4
    share = images // 4
    dp = lax.axis_index("dp")
    head = lax.axis_index("head")
    columns = heads * head_size

    both = projector.reshape(width, 2 * columns)
    own = (jnp.arange(columns) // head_size)[None, :] == jnp.arange(heads)[:, None]
    spread = jnp.where(own, jnp.tile(queries, (1, heads)), 0).astype(BF16)
    key_spec = pl.BlockSpec((width, columns), lambda i: (0, 0), memory_space=pltpu.VMEM)
    value_spec = pl.BlockSpec((width, columns), lambda i: (0, 1), memory_space=pltpu.VMEM)

    def f32(*shape):
        return jax.ShapeDtypeStruct(shape, F32)

    def bf16(*shape):
        return jax.ShapeDtypeStruct(shape, BF16)

    key_query = call(
        lambda *refs: key_query_kernel(*refs, scale=1.0 / math.sqrt(head_size)),
        f32(heads, width),
        [VMEM, key_spec],
        2 * heads * width * columns,
        2 * width * columns,
    )(spread, both)
    queried = peers([key_query] * 4)

    place = jnp.stack([dp, head]).astype(jnp.int32)
    groups = [[b * near + i for i in range(near)] for b in range(4)]

    def swap(pieces):
        return lax.all_to_all(pieces, "dp", 0, 0, axis_index_groups=groups, tiled=False)

    def across(pieces):
        return [pieces[0]] + [
            lax.ppermute(pieces[s], "dp", [(i, i ^ (s * near)) for i in range(n_dp)])
            for s in (1, 2, 3)
        ]

    text_copies = call(
        text_kernel, bf16(near, 4, width), [SMEM, VMEM, ANY], 6 << 30, 8 * n_dp * width
    )(place, captions, key_query)
    texts = swap(text_copies).reshape(near * 4, width)
    all_texts = across([texts] * 4)

    message = [bf16(heads * images, width + 128)] * 4
    mixes = call(
        lambda *refs: mix_kernel(*refs, images=images),
        message,
        [VMEM] * 5,
        64 << 30,
        3 * images * here * width,
    )(tokens, *queried)
    mixes = peers(mixes)

    embeds = call(
        lambda *refs: embed_kernel(*refs, heads=heads),
        f32(images, width),
        [VMEM] * 4 + [value_spec, VMEM],
        64 << 30,
        4 * width * columns,
    )(*mixes, both, final)
    embeds = peers([embeds] * 4)

    scalars = jnp.stack([multiplier, shift])
    unit = call(
        unit_kernel,
        bf16(images, width),
        [VMEM] * 4 + [ANY] * 3,
        8 * images * width,
        18 * images * width,
    )(*embeds, *all_texts[1:])
    units = across([unit] * 4)
    own_part, other_part = call(
        lambda *refs: image_grad_kernel(*refs, near=near),
        [f32(share, width)] * 2,
        [SMEM, SMEM] + [VMEM] * 5,
        2 * 64 * n_dp * width,
        16 * n_dp * width,
    )(place, scalars, unit, *all_texts)
    image_grad = own_part + lax.ppermute(other_part, "head", [(i, i ^ 1) for i in range(4)])
    text_part = call(
        lambda *refs: text_grad_kernel(*refs, near=near),
        bf16(near, 4 * share, width // 4),
        [SMEM, SMEM] + [VMEM] * 5 + [ANY],
        2 * 256 * near * width,
        8 * near * width,
    )(place, scalars, *units, texts, own_part)
    received = swap(text_part)
    text_grad = call(
        sum_kernel, f32(share, width), [VMEM], near * share * width, 2 * near * share * width
    )(received)
    return image_grad, text_grad


def solution(mesh):
    in_specs = (
        P("dp", "head", None),
        P(None, None, "head"),
        P("head", None),
        P("head", None),
        P("dp", None),
        P(),
        P(),
    )
    out_specs = (P(("dp", "head"), None), P(("dp", "head"), None))
    return jax.shard_map(
        per_device, mesh=mesh, in_specs=in_specs, out_specs=out_specs, check_vma=False
    )
```

```python
import math

import jax
import jax.numpy as jnp
from jax import lax
from jax.experimental import pallas as pl
from jax.experimental.pallas import tpu as pltpu
from jax.sharding import PartitionSpec as P

F32 = jnp.float32
BF16 = jnp.bfloat16
NT = (((1,), (1,)), ((), ()))
TN = (((0,), (0,)), ((), ()))
VMEM = pl.BlockSpec(memory_space=pltpu.VMEM)
ANY = pl.BlockSpec(memory_space=pl.ANY)
HBM = pl.BlockSpec(memory_space=pltpu.HBM)
SMEM = pl.BlockSpec(memory_space=pltpu.SMEM)


def call(kernel, outs, specs, flops, moved, scratch=(), out_specs=None):
    return pl.pallas_call(
        kernel,
        grid=(1,),
        out_shape=outs,
        in_specs=specs,
        out_specs=out_specs or jax.tree.map(lambda _: VMEM, outs),
        scratch_shapes=scratch,
        compiler_params=pltpu.CompilerParams(vmem_limit_bytes=12 << 20),
        cost_estimate=pl.CostEstimate(flops=flops, bytes_accessed=moved, transcendentals=0),
    )


def unit_rows(values):
    widened = values.astype(F32)
    return (widened * lax.rsqrt(jnp.sum(widened * widened, -1, keepdims=True) + 1e-06)).astype(BF16)


def peer(piece, step):
    return lax.ppermute(piece, "head", [(i, i ^ step) for i in range(4)])


def key_query_kernel(spread_ref, key_ref, out_ref, *, scale):
    out_ref[...] = (
        lax.dot_general(spread_ref[...], key_ref[...], NT, preferred_element_type=F32) * scale
    )


def mix_kernel(own_ref, other_ref, q0, q1, m0, m1, near_ref, done, *, images):
    half = images // 2
    copies = [
        pltpu.make_async_copy(
            other_ref.at[pl.ds(c * half, half)], near_ref.at[pl.ds(c * half, half)], done.at[c]
        )
        for c in range(2)
    ]
    for copy in copies:
        copy.start()
    here, width = own_ref.shape[1:]
    heads = q0.shape[0]
    spread = jnp.concatenate(
        [
            jnp.broadcast_to(ref[h : h + 1, :], (images, width))
            for ref in (q0, q1)
            for h in range(heads)
        ],
        0,
    )
    columns = spread.shape[0]
    high = spread.astype(BF16)
    low = (spread - high.astype(F32)).astype(BF16)
    both = jnp.concatenate([high, low], 0)
    own = own_ref[...].reshape(images * here, width)
    raw = [lax.dot_general(both, own, NT, preferred_element_type=F32)]
    for copy in copies:
        copy.wait()
    other = near_ref[...].reshape(images * here, width)
    raw.append(lax.dot_general(both, other, NT, preferred_element_type=F32))
    raw = jnp.concatenate(raw, 1)
    scores = raw[:columns] + raw[columns:]
    row_image = lax.broadcasted_iota(jnp.int32, scores.shape, 0) % images
    token_image = lax.broadcasted_iota(jnp.int32, scores.shape, 1) // here % images
    mine = row_image == token_image
    top = jnp.max(jnp.where(mine, scores, -jnp.inf), 1, keepdims=True)
    raised = jnp.exp(jnp.where(mine, scores - top, -jnp.inf))
    total = jnp.sum(raised, 1, keepdims=True)
    weights = (raised / total).astype(BF16)
    split = images * here
    mixed = jnp.dot(weights[:, :split], own, preferred_element_type=F32)
    mixed = mixed + jnp.dot(weights[:, split:], other, preferred_element_type=F32)
    mixed = mixed.astype(BF16)
    log_total = top + jnp.log(total)
    high = log_total.astype(BF16).astype(F32)
    middle = (log_total - high).astype(BF16).astype(F32)
    low = log_total - high - middle
    lane = lax.broadcasted_iota(jnp.int32, (columns, 128), 1)
    pieces = jnp.where(lane == 0, high, jnp.where(lane == 1, middle, jnp.where(lane == 2, low, 0.0)))
    pieces = pieces.astype(BF16)
    step = columns // 2
    for s, ref in enumerate((m0, m1)):
        ref[:, :width] = mixed[s * step : (s + 1) * step]
        ref[:, width:] = pieces[s * step : (s + 1) * step]


def embed_kernel(m0, m1, value_ref, final_ref, out_ref, *, heads):
    width = value_ref.shape[0]
    parts = (m0, m1)
    logs = [jnp.sum(ref[:, width:].astype(F32), -1, keepdims=True) for ref in parts]
    peak = jnp.maximum(logs[0], logs[1])
    shares = [jnp.exp(entry - peak) for entry in logs]
    whole = shares[0] + shares[1]
    mixed = sum((s / whole) * ref[:, :width].astype(F32) for s, ref in zip(shares, parts))
    pooled = jnp.dot(mixed.astype(BF16), value_ref[...], preferred_element_type=F32)
    rows, columns = pooled.shape
    images = rows // heads
    row_head = lax.broadcasted_iota(jnp.int32, pooled.shape, 0) // images
    column_head = lax.broadcasted_iota(jnp.int32, pooled.shape, 1) // (columns // heads)
    kept = jnp.where(row_head == column_head, pooled, 0.0)
    pooled = sum(kept[h * images : (h + 1) * images] for h in range(heads))
    out_ref[...] = jnp.dot(pooled.astype(BF16), final_ref[...], preferred_element_type=F32)


def text_kernel(place_ref, captions_ref, order_ref, out_ref):
    core = place_ref[1] % 2
    unit = unit_rows(captions_ref[...]).astype(F32)
    first = jnp.concatenate([unit[0:2], unit[4:6]], 0)
    second = jnp.concatenate([unit[2:4], unit[6:8]], 0)
    chosen = jnp.where(core == 0, first, second).astype(BF16)
    out_ref[...] = jnp.broadcast_to(chosen[None], out_ref.shape)


def rows_kernel(text_ref, order_ref, final_ref, rows_ref):
    texts = text_ref[...].astype(F32)
    rows_ref[...] = jnp.concatenate([texts[i] for i in range(texts.shape[0])], 0).astype(BF16)


def text_ids(shape, first_dp, images, head):
    column = lax.broadcasted_iota(jnp.int32, shape, 1)
    return (first_dp + column // 4) * images + column % 4 // 2 * 4 + head % 2 * 2 + column % 2


def unit_kernel(e0, e1, e2, e3, order1, order2, order3, unit_ref):
    embed = (e0[...] + e1[...]) + (e2[...] + e3[...])
    unit_ref[...] = unit_rows(embed)


def text_grad_kernel(place_ref, scalar_ref, u0, u1, u2, u3, text_ref, order_ref, part_ref, *, near):
    dp, head = place_ref[0], place_ref[1]
    multiplier, shift = scalar_ref[0], scalar_ref[1]
    images, width = u0.shape
    chunk = width // 4
    block = dp // near
    units = jnp.concatenate([ref[...].astype(F32) for ref in (u0, u1, u2, u3)], 0)
    logits = lax.dot_general(units.astype(BF16), text_ref[...], NT, preferred_element_type=F32)
    logits = logits * multiplier + shift
    row = lax.broadcasted_iota(jnp.int32, logits.shape, 0)
    image_id = ((block ^ (row // images)) * near + dp % near) * images + row % images
    text_id = text_ids(logits.shape, block * near, images, head)
    matched = jnp.where(image_id == text_id, 1.0, 0.0)
    coefficient = (multiplier * (jax.nn.sigmoid(logits) - matched)).astype(BF16)
    source = lax.broadcasted_iota(jnp.int32, (near * 4, near * 8), 0)
    target = lax.broadcasted_iota(jnp.int32, (near * 4, near * 8), 1)
    repeat = jnp.where(source == target // 8 * 4 + head // 2 * 2 + target % 8 // 4, 1.0, 0.0)
    wide = jnp.dot(coefficient, repeat.astype(BF16), preferred_element_type=F32)
    wide = jnp.concatenate([wide] * 4, 0)
    row_chunk = lax.broadcasted_iota(jnp.int32, wide.shape, 0) // (4 * images)
    column_chunk = lax.broadcasted_iota(jnp.int32, wide.shape, 1) % 4
    wide = jnp.where(row_chunk == column_chunk, wide, 0.0).astype(BF16)
    stacked = jnp.concatenate([units[:, c * chunk : (c + 1) * chunk] for c in range(4)], 0)
    part = lax.dot_general(wide, stacked.astype(BF16), TN, preferred_element_type=F32)
    part_ref[...] = part.reshape(part_ref.shape).astype(part_ref.dtype)


def image_grad_kernel(
    place_ref, scalar_ref, unit_ref, t0, t1, t2, t3, own_ref, other_ref, *, near
):
    dp, head = place_ref[0], place_ref[1]
    multiplier, shift = scalar_ref[0], scalar_ref[1]
    images, width = unit_ref.shape
    share = images // 4
    block = dp // near
    texts = [ref[...] for ref in (t0, t1, t2, t3)]
    count = texts[0].shape[0]
    logits = [
        lax.dot_general(unit_ref[...], part, NT, preferred_element_type=F32) for part in texts
    ]
    logits = jnp.concatenate(logits, 1) * multiplier + shift
    image_id = dp * images + lax.broadcasted_iota(jnp.int32, logits.shape, 0)
    column = lax.broadcasted_iota(jnp.int32, logits.shape, 1)
    first_dp = ((column // count) ^ block) * near
    text_id = (first_dp + column % count // 4) * images
    text_id = text_id + column % 4 // 2 * 4 + head % 2 * 2 + column % 2
    matched = jnp.where(image_id == text_id, 1.0, 0.0)
    coefficient = (multiplier * (jax.nn.sigmoid(logits) - matched)).astype(BF16)
    grads = sum(
        jnp.dot(coefficient[:, s * count : (s + 1) * count], part, preferred_element_type=F32)
        for s, part in enumerate(texts)
    )
    for wanted, ref in ((head, own_ref), (head ^ 1, other_ref)):
        ref[...] = sum(
            jnp.where(wanted == k, grads[k * share : (k + 1) * share], 0.0) for k in range(4)
        )


def sum_kernel(part_ref, own_ref, other_ref, image_ref, out_ref):
    image_ref[...] = own_ref[...] + other_ref[...]
    share, width = out_ref.shape
    chunk = part_ref.shape[2]
    total = jnp.sum(part_ref[...].astype(F32), 0)
    for r in range(share):
        for c in range(4):
            out_ref[r : r + 1, c * chunk : (c + 1) * chunk] = total[r * 4 + c : r * 4 + c + 1]


def per_device(tokens, projector, queries, final, captions, multiplier, shift):
    images, here, width = tokens.shape
    heads, head_size = queries.shape
    n_dp = lax.axis_size("dp")
    near = n_dp // 4
    share = images // 4
    dp = lax.axis_index("dp")
    head = lax.axis_index("head")
    columns = heads * head_size

    both = projector.reshape(width, 2 * columns)
    own = (jnp.arange(columns) // head_size)[None, :] == jnp.arange(heads)[:, None]
    spread = jnp.where(own, jnp.tile(queries, (1, heads)), 0).astype(BF16)
    key_spec = pl.BlockSpec((width, columns), lambda i: (0, 0), memory_space=pltpu.VMEM)
    value_spec = pl.BlockSpec((width, columns), lambda i: (0, 1), memory_space=pltpu.VMEM)

    def f32(*shape):
        return jax.ShapeDtypeStruct(shape, F32)

    def bf16(*shape):
        return jax.ShapeDtypeStruct(shape, BF16)

    other_tokens = peer(tokens, 1)
    key_query = call(
        lambda *refs: key_query_kernel(*refs, scale=1.0 / math.sqrt(head_size)),
        f32(heads, width),
        [VMEM, key_spec],
        2 * heads * width * columns,
        2 * width * columns,
    )(spread, both)

    place = jnp.stack([dp, head]).astype(jnp.int32)
    groups = [[b * near + i for i in range(near)] for b in range(4)]

    def swap(pieces):
        return lax.all_to_all(pieces, "dp", 0, 0, axis_index_groups=groups, tiled=False)

    def across(pieces):
        return [pieces[0]] + [
            lax.ppermute(pieces[s], "dp", [(i, i ^ (s * near)) for i in range(n_dp)])
            for s in (1, 2, 3)
        ]

    text_copies = call(
        text_kernel, bf16(near, 4, width), [SMEM, VMEM, ANY], 6 << 30, 8 * n_dp * width
    )(place, captions, key_query)
    copies = swap(text_copies)

    mixes = call(
        lambda *refs: mix_kernel(*refs, images=images),
        [bf16(heads * images, width + 128)] * 2,
        [VMEM, ANY, VMEM, VMEM],
        64 << 30,
        6 * images * here * width,
        [pltpu.VMEM(tokens.shape, BF16), pltpu.SemaphoreType.DMA((2,))],
    )(tokens, other_tokens, key_query, peer(key_query, 2))
    texts = call(
        rows_kernel, bf16(near * 4, width), [VMEM, ANY, ANY], near * 4 * width, 16 * near * width
    )(copies, mixes[0], final)
    all_texts = across([texts] * 4)
    embeds = call(
        lambda *refs: embed_kernel(*refs, heads=heads),
        f32(images, width),
        [VMEM, VMEM, value_spec, VMEM],
        64 << 30,
        4 * width * columns,
    )(mixes[0], peer(mixes[1], 2), both, final)
    embeds = [embeds] + [peer(embeds, s) for s in (1, 2, 3)]

    scalars = jnp.stack([multiplier, shift])
    unit = call(
        unit_kernel,
        bf16(images, width),
        [VMEM] * 4 + [ANY] * 3,
        8 * images * width,
        18 * images * width,
    )(*embeds, *all_texts[1:])
    units = across([unit] * 4)
    own_part, other_part = call(
        lambda *refs: image_grad_kernel(*refs, near=near),
        [f32(share, width)] * 2,
        [SMEM, SMEM] + [VMEM] * 5,
        2 * 64 * n_dp * width,
        16 * n_dp * width,
    )(place, scalars, unit, *all_texts)
    other_part = peer(other_part, 1)
    text_part = call(
        lambda *refs: text_grad_kernel(*refs, near=near),
        bf16(near, 4 * share, width // 4),
        [SMEM, SMEM] + [VMEM] * 5 + [ANY],
        2 * 256 * near * width,
        8 * near * width,
    )(place, scalars, *units, texts, own_part)
    received = swap(text_part)
    image_grad, text_grad = call(
        sum_kernel, [f32(share, width)] * 2, [VMEM] * 3, near * share * width, 2 * near * share * width
    )(received, own_part, other_part)
    return image_grad, text_grad


def solution(mesh):
    in_specs = (
        P("dp", "head", None),
        P(None, None, "head"),
        P("head", None),
        P("head", None),
        P("dp", None),
        P(),
        P(),
    )
    out_specs = (P(("dp", "head"), None), P(("dp", "head"), None))
    return jax.shard_map(
        per_device, mesh=mesh, in_specs=in_specs, out_specs=out_specs, check_vma=False
    )
```

```python
import math

import jax
import jax.numpy as jnp
from jax import lax
from jax.experimental import pallas as pl
from jax.experimental.pallas import tpu as pltpu
from jax.sharding import PartitionSpec as P

F32 = jnp.float32
BF16 = jnp.bfloat16
NT = (((1,), (1,)), ((), ()))
TN = (((0,), (0,)), ((), ()))
VMEM = pl.BlockSpec(memory_space=pltpu.VMEM)
ANY = pl.BlockSpec(memory_space=pl.ANY)
HBM = pl.BlockSpec(memory_space=pltpu.HBM)
SMEM = pl.BlockSpec(memory_space=pltpu.SMEM)


def call(kernel, outs, specs, flops, moved, scratch=(), limit=12):
    return pl.pallas_call(
        kernel,
        grid=(1,),
        out_shape=outs,
        in_specs=specs,
        out_specs=jax.tree.map(lambda _: VMEM, outs),
        scratch_shapes=scratch,
        compiler_params=pltpu.CompilerParams(vmem_limit_bytes=limit << 20),
        cost_estimate=pl.CostEstimate(flops=flops, bytes_accessed=moved, transcendentals=0),
    )


def unit_rows(values):
    widened = values.astype(F32)
    return (widened * lax.rsqrt(jnp.sum(widened * widened, -1, keepdims=True) + 1e-06)).astype(BF16)


def peer(piece, step):
    return lax.ppermute(piece, "head", [(i, i ^ step) for i in range(4)])


def key_query_kernel(spread_ref, key_ref, out_ref, *, scale):
    out_ref[...] = (
        lax.dot_general(spread_ref[...], key_ref[...], NT, preferred_element_type=F32) * scale
    )


def mix_kernel(own_ref, other_ref, q0, q1, m0, m1, near_ref, done, *, images):
    copies = [
        pltpu.make_async_copy(ref, near_ref.at[i], done.at[i])
        for i, ref in enumerate((own_ref, other_ref))
    ]
    for copy in copies:
        copy.start()
    here, width = own_ref.shape[1:]
    heads = q0.shape[0]
    spread = jnp.concatenate(
        [
            jnp.broadcast_to(ref[h : h + 1, :], (images, width))
            for ref in (q0, q1)
            for h in range(heads)
        ],
        0,
    )
    columns = spread.shape[0]
    high = spread.astype(BF16)
    low = (spread - high.astype(F32)).astype(BF16)
    both = jnp.concatenate([high, low], 0)
    sides, raw = [], []
    for i, copy in enumerate(copies):
        copy.wait()
        sides.append(near_ref[i].reshape(images * here, width))
        raw.append(lax.dot_general(both, sides[i], NT, preferred_element_type=F32))
    raw = jnp.concatenate(raw, 1)
    scores = raw[:columns] + raw[columns:]
    row_image = lax.broadcasted_iota(jnp.int32, scores.shape, 0) % images
    token_image = lax.broadcasted_iota(jnp.int32, scores.shape, 1) // here % images
    mine = row_image == token_image
    top = jnp.max(jnp.where(mine, scores, -jnp.inf), 1, keepdims=True)
    raised = jnp.exp(jnp.where(mine, scores - top, -jnp.inf))
    total = jnp.sum(raised, 1, keepdims=True)
    weights = (raised / total).astype(BF16)
    split = images * here
    mixed = jnp.dot(weights[:, :split], sides[0], preferred_element_type=F32)
    mixed = mixed + jnp.dot(weights[:, split:], sides[1], preferred_element_type=F32)
    mixed = mixed.astype(BF16)
    log_total = top + jnp.log(total)
    high = log_total.astype(BF16).astype(F32)
    middle = (log_total - high).astype(BF16).astype(F32)
    low = log_total - high - middle
    lane = lax.broadcasted_iota(jnp.int32, (columns, 128), 1)
    pieces = jnp.where(lane == 0, high, jnp.where(lane == 1, middle, jnp.where(lane == 2, low, 0.0)))
    pieces = pieces.astype(BF16)
    step = columns // 2
    for s, ref in enumerate((m0, m1)):
        ref[:, :width] = mixed[s * step : (s + 1) * step]
        ref[:, width:] = pieces[s * step : (s + 1) * step]


def embed_kernel(m0, m1, value_ref, final_ref, out_ref, near_ref, done, *, heads):
    copy = pltpu.make_async_copy(final_ref, near_ref, done)
    copy.start()
    width = value_ref.shape[0]
    parts = (m0, m1)
    logs = [jnp.sum(ref[:, width:].astype(F32), -1, keepdims=True) for ref in parts]
    peak = jnp.maximum(logs[0], logs[1])
    shares = [jnp.exp(entry - peak) for entry in logs]
    whole = shares[0] + shares[1]
    mixed = sum((s / whole) * ref[:, :width].astype(F32) for s, ref in zip(shares, parts))
    pooled = jnp.dot(mixed.astype(BF16), value_ref[...], preferred_element_type=F32)
    rows, columns = pooled.shape
    images = rows // heads
    row_head = lax.broadcasted_iota(jnp.int32, pooled.shape, 0) // images
    column_head = lax.broadcasted_iota(jnp.int32, pooled.shape, 1) // (columns // heads)
    kept = jnp.where(row_head == column_head, pooled, 0.0)
    pooled = sum(kept[h * images : (h + 1) * images] for h in range(heads))
    copy.wait()
    out_ref[...] = jnp.dot(pooled.astype(BF16), near_ref[...], preferred_element_type=F32)


def text_kernel(place_ref, captions_ref, order_ref, out_ref):
    core = place_ref[1] % 2
    unit = unit_rows(captions_ref[...]).astype(F32)
    first = jnp.concatenate([unit[0:2], unit[4:6]], 0)
    second = jnp.concatenate([unit[2:4], unit[6:8]], 0)
    chosen = jnp.where(core == 0, first, second).astype(BF16)
    out_ref[...] = jnp.broadcast_to(chosen[None], out_ref.shape)


def rows_kernel(text_ref, order_ref, rows_ref):
    texts = text_ref[...].astype(F32)
    rows_ref[...] = jnp.concatenate([texts[i] for i in range(texts.shape[0])], 0).astype(BF16)


def text_ids(shape, first_dp, images, head):
    column = lax.broadcasted_iota(jnp.int32, shape, 1)
    return (first_dp + column // 4) * images + column % 4 // 2 * 4 + head % 2 * 2 + column % 2


def unit_kernel(e0, e1, e2, e3, order1, order2, order3, unit_ref):
    embed = (e0[...] + e1[...]) + (e2[...] + e3[...])
    unit_ref[...] = unit_rows(embed)


def text_grad_kernel(place_ref, scalar_ref, u0, u1, u2, u3, text_ref, order_ref, part_ref, *, near):
    dp, head = place_ref[0], place_ref[1]
    multiplier, shift = scalar_ref[0], scalar_ref[1]
    images, width = u0.shape
    chunk = width // 4
    block = dp // near
    units = jnp.concatenate([ref[...].astype(F32) for ref in (u0, u1, u2, u3)], 0)
    logits = lax.dot_general(units.astype(BF16), text_ref[...], NT, preferred_element_type=F32)
    logits = logits * multiplier + shift
    row = lax.broadcasted_iota(jnp.int32, logits.shape, 0)
    image_id = ((block ^ (row // images)) * near + dp % near) * images + row % images
    text_id = text_ids(logits.shape, block * near, images, head)
    matched = jnp.where(image_id == text_id, 1.0, 0.0)
    coefficient = (multiplier * (jax.nn.sigmoid(logits) - matched)).astype(BF16)
    source = lax.broadcasted_iota(jnp.int32, (near * 4, near * 8), 0)
    target = lax.broadcasted_iota(jnp.int32, (near * 4, near * 8), 1)
    repeat = jnp.where(source == target // 8 * 4 + head // 2 * 2 + target % 8 // 4, 1.0, 0.0)
    wide = jnp.dot(coefficient, repeat.astype(BF16), preferred_element_type=F32)
    wide = jnp.concatenate([wide] * 4, 0)
    row_chunk = lax.broadcasted_iota(jnp.int32, wide.shape, 0) // (4 * images)
    column_chunk = lax.broadcasted_iota(jnp.int32, wide.shape, 1) % 4
    wide = jnp.where(row_chunk == column_chunk, wide, 0.0).astype(BF16)
    stacked = jnp.concatenate([units[:, c * chunk : (c + 1) * chunk] for c in range(4)], 0)
    part = lax.dot_general(wide, stacked.astype(BF16), TN, preferred_element_type=F32)
    part_ref[...] = part.reshape(part_ref.shape).astype(part_ref.dtype)


def image_grad_kernel(
    place_ref, scalar_ref, unit_ref, t0, t1, t2, t3, own_ref, other_ref, *, near
):
    dp, head = place_ref[0], place_ref[1]
    multiplier, shift = scalar_ref[0], scalar_ref[1]
    images, width = unit_ref.shape
    share = images // 4
    block = dp // near
    texts = [ref[...] for ref in (t0, t1, t2, t3)]
    count = texts[0].shape[0]
    logits = [
        lax.dot_general(unit_ref[...], part, NT, preferred_element_type=F32) for part in texts
    ]
    logits = jnp.concatenate(logits, 1) * multiplier + shift
    image_id = dp * images + lax.broadcasted_iota(jnp.int32, logits.shape, 0)
    column = lax.broadcasted_iota(jnp.int32, logits.shape, 1)
    first_dp = ((column // count) ^ block) * near
    text_id = (first_dp + column % count // 4) * images
    text_id = text_id + column % 4 // 2 * 4 + head % 2 * 2 + column % 2
    matched = jnp.where(image_id == text_id, 1.0, 0.0)
    coefficient = (multiplier * (jax.nn.sigmoid(logits) - matched)).astype(BF16)
    grads = sum(
        jnp.dot(coefficient[:, s * count : (s + 1) * count], part, preferred_element_type=F32)
        for s, part in enumerate(texts)
    )
    for wanted, ref in ((head, own_ref), (head ^ 1, other_ref)):
        ref[...] = sum(
            jnp.where(wanted == k, grads[k * share : (k + 1) * share], 0.0) for k in range(4)
        )


def sum_kernel(part_ref, own_ref, other_ref, image_ref, out_ref):
    image_ref[...] = own_ref[...] + other_ref[...]
    share, width = out_ref.shape
    chunk = part_ref.shape[2]
    total = jnp.sum(part_ref[...].astype(F32), 0)
    for r in range(share):
        for c in range(4):
            out_ref[r : r + 1, c * chunk : (c + 1) * chunk] = total[r * 4 + c : r * 4 + c + 1]


def per_device(tokens, projector, queries, final, captions, multiplier, shift):
    images, here, width = tokens.shape
    heads, head_size = queries.shape
    n_dp = lax.axis_size("dp")
    near = n_dp // 4
    share = images // 4
    dp = lax.axis_index("dp")
    head = lax.axis_index("head")
    columns = heads * head_size

    both = projector.reshape(width, 2 * columns)
    own = (jnp.arange(columns) // head_size)[None, :] == jnp.arange(heads)[:, None]
    spread = jnp.where(own, jnp.tile(queries, (1, heads)), 0).astype(BF16)
    key_spec = pl.BlockSpec((width, columns), lambda i: (0, 0), memory_space=pltpu.VMEM)
    value_spec = pl.BlockSpec((width, columns), lambda i: (0, 1), memory_space=pltpu.VMEM)

    def f32(*shape):
        return jax.ShapeDtypeStruct(shape, F32)

    def bf16(*shape):
        return jax.ShapeDtypeStruct(shape, BF16)

    other_tokens = peer(tokens, 1)
    key_query = call(
        lambda *refs: key_query_kernel(*refs, scale=1.0 / math.sqrt(head_size)),
        f32(heads, width),
        [VMEM, key_spec],
        2 * heads * width * columns,
        2 * width * columns,
    )(spread, both)

    place = jnp.stack([dp, head]).astype(jnp.int32)
    groups = [[b * near + i for i in range(near)] for b in range(4)]

    def swap(pieces):
        return lax.all_to_all(pieces, "dp", 0, 0, axis_index_groups=groups, tiled=False)

    def across(pieces):
        return [pieces[0]] + [
            lax.ppermute(pieces[s], "dp", [(i, i ^ (s * near)) for i in range(n_dp)])
            for s in (1, 2, 3)
        ]

    text_copies = call(
        text_kernel, bf16(near, 4, width), [SMEM, VMEM, ANY], 6 << 30, 8 * n_dp * width
    )(place, captions, key_query)
    copies = swap(text_copies)

    mixes = call(
        lambda *refs: mix_kernel(*refs, images=images),
        [bf16(heads * images, width + 128)] * 2,
        [ANY, ANY, VMEM, VMEM],
        64 << 30,
        6 * images * here * width,
        [pltpu.VMEM((2, *tokens.shape), BF16), pltpu.SemaphoreType.DMA((2,))],
        53,
    )(tokens, other_tokens, key_query, peer(key_query, 2))
    texts = call(
        rows_kernel, bf16(near * 4, width), [VMEM, ANY], near * 4 * width, 16 * near * width
    )(copies, mixes[0])
    all_texts = across([texts] * 4)
    embeds = call(
        lambda *refs: embed_kernel(*refs, heads=heads),
        f32(images, width),
        [VMEM, VMEM, value_spec, ANY],
        64 << 30,
        4 * width * columns,
        [pltpu.VMEM(final.shape, BF16), pltpu.SemaphoreType.DMA],
        52,
    )(mixes[0], peer(mixes[1], 2), both, final)
    embeds = [embeds] + [peer(embeds, s) for s in (1, 2, 3)]

    scalars = jnp.stack([multiplier, shift])
    unit = call(
        unit_kernel,
        bf16(images, width),
        [VMEM] * 4 + [ANY] * 3,
        8 * images * width,
        18 * images * width,
    )(*embeds, *all_texts[1:])
    units = across([unit] * 4)
    own_part, other_part = call(
        lambda *refs: image_grad_kernel(*refs, near=near),
        [f32(share, width)] * 2,
        [SMEM, SMEM] + [VMEM] * 5,
        2 * 64 * n_dp * width,
        16 * n_dp * width,
    )(place, scalars, unit, *all_texts)
    other_part = peer(other_part, 1)
    text_part = call(
        lambda *refs: text_grad_kernel(*refs, near=near),
        bf16(near, 4 * share, width // 4),
        [SMEM, SMEM] + [VMEM] * 5 + [ANY],
        2 * 256 * near * width,
        8 * near * width,
    )(place, scalars, *units, texts, other_part)
    received = swap(text_part)
    image_grad, text_grad = call(
        sum_kernel, [f32(share, width)] * 2, [VMEM] * 3, near * share * width, 2 * near * share * width
    )(received, own_part, other_part)
    return image_grad, text_grad


def solution(mesh):
    in_specs = (
        P("dp", "head", None),
        P(None, None, "head"),
        P("head", None),
        P("head", None),
        P("dp", None),
        P(),
        P(),
    )
    out_specs = (P(("dp", "head"), None), P(("dp", "head"), None))
    return jax.shard_map(
        per_device, mesh=mesh, in_specs=in_specs, out_specs=out_specs, check_vma=False
    )
```

```python
import math

import jax
import jax.numpy as jnp
from jax import lax
from jax.experimental import pallas as pl
from jax.experimental.pallas import tpu as pltpu
from jax.sharding import PartitionSpec as P

F32 = jnp.float32
BF16 = jnp.bfloat16
NT = (((1,), (1,)), ((), ()))
TN = (((0,), (0,)), ((), ()))
VMEM = pl.BlockSpec(memory_space=pltpu.VMEM)
ANY = pl.BlockSpec(memory_space=pl.ANY)
HBM = pl.BlockSpec(memory_space=pltpu.HBM)
SMEM = pl.BlockSpec(memory_space=pltpu.SMEM)


def call(kernel, outs, specs, flops, moved, scratch=(), limit=12):
    return pl.pallas_call(
        kernel,
        grid=(1,),
        out_shape=outs,
        in_specs=specs,
        out_specs=jax.tree.map(lambda _: VMEM, outs),
        scratch_shapes=scratch,
        compiler_params=pltpu.CompilerParams(vmem_limit_bytes=limit << 20),
        cost_estimate=pl.CostEstimate(flops=flops, bytes_accessed=moved, transcendentals=0),
    )


def unit_rows(values):
    widened = values.astype(F32)
    return (widened * lax.rsqrt(jnp.sum(widened * widened, -1, keepdims=True) + 1e-06)).astype(BF16)


def peer(piece, step):
    return lax.ppermute(piece, "head", [(i, i ^ step) for i in range(4)])


def key_query_kernel(spread_ref, key_ref, out_ref, *, scale):
    out_ref[...] = (
        lax.dot_general(spread_ref[...], key_ref[...], NT, preferred_element_type=F32) * scale
    )


def mix_kernel(own_ref, other_ref, q0, q1, m0, m1, near_ref, done, *, images):
    copies = [
        pltpu.make_async_copy(ref, near_ref.at[i], done.at[i])
        for i, ref in enumerate((own_ref, other_ref))
    ]
    for copy in copies:
        copy.start()
    here, width = own_ref.shape[1:]
    heads = q0.shape[0]
    spread = jnp.concatenate(
        [
            jnp.broadcast_to(ref[h : h + 1, :], (images, width))
            for ref in (q0, q1)
            for h in range(heads)
        ],
        0,
    )
    columns = spread.shape[0]
    high = spread.astype(BF16)
    low = (spread - high.astype(F32)).astype(BF16)
    both = jnp.concatenate([high, low], 0)
    sides, raw = [], []
    for i, copy in enumerate(copies):
        copy.wait()
        sides.append(near_ref[i].reshape(images * here, width))
        raw.append(lax.dot_general(both, sides[i], NT, preferred_element_type=F32))
    raw = jnp.concatenate(raw, 1)
    scores = raw[:columns] + raw[columns:]
    row_image = lax.broadcasted_iota(jnp.int32, scores.shape, 0) % images
    token_image = lax.broadcasted_iota(jnp.int32, scores.shape, 1) // here % images
    mine = row_image == token_image
    top = jnp.max(jnp.where(mine, scores, -jnp.inf), 1, keepdims=True)
    raised = jnp.exp(jnp.where(mine, scores - top, -jnp.inf))
    total = jnp.sum(raised, 1, keepdims=True)
    weights = (raised / total).astype(BF16)
    split = images * here
    mixed = jnp.dot(weights[:, :split], sides[0], preferred_element_type=F32)
    mixed = mixed + jnp.dot(weights[:, split:], sides[1], preferred_element_type=F32)
    mixed = mixed.astype(BF16)
    log_total = top + jnp.log(total)
    high = log_total.astype(BF16).astype(F32)
    middle = (log_total - high).astype(BF16).astype(F32)
    low = log_total - high - middle
    lane = lax.broadcasted_iota(jnp.int32, (columns, 128), 1)
    pieces = jnp.where(lane == 0, high, jnp.where(lane == 1, middle, jnp.where(lane == 2, low, 0.0)))
    pieces = pieces.astype(BF16)
    step = columns // 2
    for s, ref in enumerate((m0, m1)):
        ref[:, :width] = mixed[s * step : (s + 1) * step]
        ref[:, width:] = pieces[s * step : (s + 1) * step]


def embed_kernel(m0, m1, value_ref, final_ref, out_ref, *, heads):
    width = value_ref.shape[0]
    parts = (m0, m1)
    logs = [jnp.sum(ref[:, width:].astype(F32), -1, keepdims=True) for ref in parts]
    peak = jnp.maximum(logs[0], logs[1])
    shares = [jnp.exp(entry - peak) for entry in logs]
    whole = shares[0] + shares[1]
    mixed = sum((s / whole) * ref[:, :width].astype(F32) for s, ref in zip(shares, parts))
    pooled = jnp.dot(mixed.astype(BF16), value_ref[...], preferred_element_type=F32)
    rows, columns = pooled.shape
    images = rows // heads
    row_head = lax.broadcasted_iota(jnp.int32, pooled.shape, 0) // images
    column_head = lax.broadcasted_iota(jnp.int32, pooled.shape, 1) // (columns // heads)
    kept = jnp.where(row_head == column_head, pooled, 0.0)
    pooled = sum(kept[h * images : (h + 1) * images] for h in range(heads))
    out_ref[...] = jnp.dot(pooled.astype(BF16), final_ref[...], preferred_element_type=F32)


def text_kernel(place_ref, captions_ref, order_ref, out_ref):
    core = place_ref[1] % 2
    unit = unit_rows(captions_ref[...]).astype(F32)
    first = jnp.concatenate([unit[0:2], unit[4:6]], 0)
    second = jnp.concatenate([unit[2:4], unit[6:8]], 0)
    chosen = jnp.where(core == 0, first, second).astype(BF16)
    out_ref[...] = jnp.broadcast_to(chosen[None], out_ref.shape)


def rows_kernel(text_ref, order_ref, rows_ref):
    texts = text_ref[...].astype(F32)
    rows_ref[...] = jnp.concatenate([texts[i] for i in range(texts.shape[0])], 0).astype(BF16)


def text_ids(shape, first_dp, images, head):
    column = lax.broadcasted_iota(jnp.int32, shape, 1)
    local = column // 4 * 7 % 16
    return (first_dp + local) * images + column % 4 // 2 * 4 + head % 2 * 2 + column % 2


def unit_kernel(e0, e1, e2, e3, order1, order2, order3, unit_ref):
    embed = (e0[...] + e1[...]) + (e2[...] + e3[...])
    unit_ref[...] = unit_rows(embed)


def text_grad_kernel(place_ref, scalar_ref, u0, u1, u2, u3, text_ref, order_ref, part_ref, *, near):
    dp, head = place_ref[0], place_ref[1]
    multiplier, shift = scalar_ref[0], scalar_ref[1]
    images, width = u0.shape
    chunk = width // 4
    block = dp // near
    units = jnp.concatenate([ref[...].astype(F32) for ref in (u0, u1, u2, u3)], 0)
    logits = lax.dot_general(units.astype(BF16), text_ref[...], NT, preferred_element_type=F32)
    logits = logits * multiplier + shift
    row = lax.broadcasted_iota(jnp.int32, logits.shape, 0)
    image_id = ((block ^ (row // images)) * near + dp % near) * images + row % images
    text_id = text_ids(logits.shape, block * near, images, head)
    matched = jnp.where(image_id == text_id, 1.0, 0.0)
    coefficient = (multiplier * (jax.nn.sigmoid(logits) - matched)).astype(BF16)
    source = lax.broadcasted_iota(jnp.int32, (near * 4, near * 8), 0)
    target = lax.broadcasted_iota(jnp.int32, (near * 4, near * 8), 1)
    repeat = jnp.where(source == target // 8 * 4 + head // 2 * 2 + target % 8 // 4, 1.0, 0.0)
    wide = jnp.dot(coefficient, repeat.astype(BF16), preferred_element_type=F32)
    wide = jnp.concatenate([wide] * 4, 0)
    row_chunk = lax.broadcasted_iota(jnp.int32, wide.shape, 0) // (4 * images)
    column_chunk = lax.broadcasted_iota(jnp.int32, wide.shape, 1) % 4
    wide = jnp.where(row_chunk == column_chunk, wide, 0.0).astype(BF16)
    stacked = jnp.concatenate([units[:, c * chunk : (c + 1) * chunk] for c in range(4)], 0)
    part = lax.dot_general(wide, stacked.astype(BF16), TN, preferred_element_type=F32)
    part_ref[...] = part.reshape(part_ref.shape).astype(part_ref.dtype)


def image_grad_kernel(
    place_ref, scalar_ref, unit_ref, t0, t1, t2, t3, own_ref, other_ref, *, near
):
    dp, head = place_ref[0], place_ref[1]
    multiplier, shift = scalar_ref[0], scalar_ref[1]
    images, width = unit_ref.shape
    share = images // 4
    block = dp // near
    texts = [ref[...] for ref in (t0, t1, t2, t3)]
    count = texts[0].shape[0]
    logits = [
        lax.dot_general(unit_ref[...], part, NT, preferred_element_type=F32) for part in texts
    ]
    logits = jnp.concatenate(logits, 1) * multiplier + shift
    image_id = dp * images + lax.broadcasted_iota(jnp.int32, logits.shape, 0)
    column = lax.broadcasted_iota(jnp.int32, logits.shape, 1)
    first_dp = ((column // count) ^ block) * near
    text_id = (first_dp + column % count // 4 * 7 % near) * images
    text_id = text_id + column % 4 // 2 * 4 + head % 2 * 2 + column % 2
    matched = jnp.where(image_id == text_id, 1.0, 0.0)
    coefficient = (multiplier * (jax.nn.sigmoid(logits) - matched)).astype(BF16)
    grads = sum(
        jnp.dot(coefficient[:, s * count : (s + 1) * count], part, preferred_element_type=F32)
        for s, part in enumerate(texts)
    )
    for wanted, ref in ((head, own_ref), (head ^ 1, other_ref)):
        ref[...] = sum(
            jnp.where(wanted == k, grads[k * share : (k + 1) * share], 0.0) for k in range(4)
        )


def sum_kernel(part_ref, own_ref, other_ref, image_ref, out_ref):
    image_ref[...] = own_ref[...] + other_ref[...]
    share, width = out_ref.shape
    chunk = part_ref.shape[2]
    total = jnp.sum(part_ref[...].astype(F32), 0)
    for r in range(share):
        for c in range(4):
            out_ref[r : r + 1, c * chunk : (c + 1) * chunk] = total[r * 4 + c : r * 4 + c + 1]


def per_device(tokens, projector, queries, final, captions, multiplier, shift):
    images, here, width = tokens.shape
    heads, head_size = queries.shape
    n_dp = lax.axis_size("dp")
    near = n_dp // 4
    share = images // 4
    dp = lax.axis_index("dp")
    head = lax.axis_index("head")
    columns = heads * head_size

    both = projector.reshape(width, 2 * columns)
    own = (jnp.arange(columns) // head_size)[None, :] == jnp.arange(heads)[:, None]
    spread = jnp.where(own, jnp.tile(queries, (1, heads)), 0).astype(BF16)
    key_spec = pl.BlockSpec((width, columns), lambda i: (0, 0), memory_space=pltpu.VMEM)
    value_spec = pl.BlockSpec((width, columns), lambda i: (0, 1), memory_space=pltpu.VMEM)

    def f32(*shape):
        return jax.ShapeDtypeStruct(shape, F32)

    def bf16(*shape):
        return jax.ShapeDtypeStruct(shape, BF16)

    other_tokens = peer(tokens, 1)
    key_query = call(
        lambda *refs: key_query_kernel(*refs, scale=1.0 / math.sqrt(head_size)),
        f32(heads, width),
        [VMEM, key_spec],
        2 * heads * width * columns,
        2 * width * columns,
    )(spread, both)

    place = jnp.stack([dp, head]).astype(jnp.int32)
    groups = [[b * near + i * 7 % near for i in range(near)] for b in range(4)]

    def swap(pieces):
        return lax.all_to_all(pieces, "dp", 0, 0, axis_index_groups=groups, tiled=False)

    def across(pieces):
        return [pieces[0]] + [
            lax.ppermute(pieces[s], "dp", [(i, i ^ (s * near)) for i in range(n_dp)])
            for s in (1, 2, 3)
        ]

    text_copies = call(
        text_kernel, bf16(near, 4, width), [SMEM, VMEM, ANY], 6 << 30, 8 * n_dp * width
    )(place, captions, key_query)
    copies = swap(text_copies)

    mixes = call(
        lambda *refs: mix_kernel(*refs, images=images),
        [bf16(heads * images, width + 128)] * 2,
        [ANY, ANY, VMEM, VMEM],
        64 << 30,
        6 * images * here * width,
        [pltpu.VMEM((2, *tokens.shape), BF16), pltpu.SemaphoreType.DMA((2,))],
        53,
    )(tokens, other_tokens, key_query, peer(key_query, 2))
    texts = call(
        rows_kernel, bf16(near * 4, width), [VMEM, ANY], near * 4 * width, 16 * near * width
    )(copies, mixes[0])
    all_texts = across([texts] * 4)
    embeds = call(
        lambda *refs: embed_kernel(*refs, heads=heads),
        f32(images, width),
        [VMEM, VMEM, value_spec, VMEM],
        64 << 30,
        4 * width * columns,
    )(mixes[0], peer(mixes[1], 2), both, final)
    embeds = [embeds] + [peer(embeds, s) for s in (1, 2, 3)]

    scalars = jnp.stack([multiplier, shift])
    unit = call(
        unit_kernel,
        bf16(images, width),
        [VMEM] * 4 + [ANY] * 3,
        8 * images * width,
        18 * images * width,
    )(*embeds, *all_texts[1:])
    units = across([unit] * 4)
    own_part, other_part = call(
        lambda *refs: image_grad_kernel(*refs, near=near),
        [f32(share, width)] * 2,
        [SMEM, SMEM] + [VMEM] * 5,
        2 * 64 * n_dp * width,
        16 * n_dp * width,
    )(place, scalars, unit, *all_texts)
    other_part = peer(other_part, 1)
    text_part = call(
        lambda *refs: text_grad_kernel(*refs, near=near),
        bf16(near, 4 * share, width // 4),
        [SMEM, SMEM] + [VMEM] * 5 + [ANY],
        2 * 256 * near * width,
        8 * near * width,
    )(place, scalars, *units, texts, other_part)
    received = swap(text_part)
    image_grad, text_grad = call(
        sum_kernel, [f32(share, width)] * 2, [VMEM] * 3, near * share * width, 2 * near * share * width
    )(received, own_part, other_part)
    return image_grad, text_grad


def solution(mesh):
    in_specs = (
        P("dp", "head", None),
        P(None, None, "head"),
        P("head", None),
        P("head", None),
        P("dp", None),
        P(),
        P(),
    )
    out_specs = (P(("dp", "head"), None), P(("dp", "head"), None))
    return jax.shard_map(
        per_device, mesh=mesh, in_specs=in_specs, out_specs=out_specs, check_vma=False
    )
```

```python
import math

import jax
import jax.numpy as jnp
from jax import lax
from jax.experimental import pallas as pl
from jax.experimental.pallas import tpu as pltpu
from jax.sharding import PartitionSpec as P

F32 = jnp.float32
BF16 = jnp.bfloat16
NT = (((1,), (1,)), ((), ()))
TN = (((0,), (0,)), ((), ()))
VMEM = pl.BlockSpec(memory_space=pltpu.VMEM)
ANY = pl.BlockSpec(memory_space=pl.ANY)
HBM = pl.BlockSpec(memory_space=pltpu.HBM)
SMEM = pl.BlockSpec(memory_space=pltpu.SMEM)


def call(kernel, outs, specs, flops, moved, scratch=(), limit=12, out_specs=None):
    return pl.pallas_call(
        kernel,
        grid=(1,),
        out_shape=outs,
        in_specs=specs,
        out_specs=out_specs or jax.tree.map(lambda _: VMEM, outs),
        scratch_shapes=scratch,
        compiler_params=pltpu.CompilerParams(vmem_limit_bytes=limit << 20),
        cost_estimate=pl.CostEstimate(flops=flops, bytes_accessed=moved, transcendentals=0),
    )


def unit_rows(values):
    widened = values.astype(F32)
    return (widened * lax.rsqrt(jnp.sum(widened * widened, -1, keepdims=True) + 1e-06)).astype(BF16)


def peer(piece, step):
    return lax.ppermute(piece, "head", [(i, i ^ step) for i in range(4)])


def first_kernel(
    place_ref, spread_ref, key_ref, captions_ref, query_ref, text_ref, copies_ref, done, *, scale
):
    core = place_ref[1] % 2
    unit = unit_rows(captions_ref[...]).astype(F32)
    first = jnp.concatenate([unit[0:2], unit[4:6]], 0)
    second = jnp.concatenate([unit[2:4], unit[6:8]], 0)
    chosen = jnp.where(core == 0, first, second)
    half = chosen.shape[1] // 2
    chosen = jnp.concatenate([chosen[:, :half], chosen[:, half:]], 0).astype(BF16)
    copies_ref[...] = jnp.broadcast_to(chosen[None], copies_ref.shape)
    copy = pltpu.make_async_copy(copies_ref, text_ref, done)
    copy.start()
    query_ref[...] = (
        lax.dot_general(spread_ref[...], key_ref[...], NT, preferred_element_type=F32) * scale
    )
    copy.wait()


def halves_product(units, texts):
    half = texts.shape[1]
    low = lax.dot_general(units[:, :half], texts, NT, preferred_element_type=F32)
    high = lax.dot_general(units[:, half:], texts, NT, preferred_element_type=F32)
    upper = lax.broadcasted_iota(jnp.int32, low.shape, 1) % 8 // 4 == 1
    own = jnp.where(upper, high, low)
    count = own.shape[1]
    return own + jnp.where(upper, pltpu.roll(own, 4, 1), pltpu.roll(own, count - 4, 1))


def text_ids(shape, first_dp, images, head):
    column = lax.broadcasted_iota(jnp.int32, shape, 1)
    local = column // 8 * 7 % 16
    return (first_dp + local) * images + column % 4 // 2 * 4 + head % 2 * 2 + column % 2


def mix_kernel(own_ref, other_ref, q0, q1, m0, m1, near_ref, done, *, images):
    copies = [
        pltpu.make_async_copy(ref, near_ref.at[i], done.at[i])
        for i, ref in enumerate((own_ref, other_ref))
    ]
    for copy in copies:
        copy.start()
    here, width = own_ref.shape[1:]
    heads = q0.shape[0]
    spread = jnp.concatenate(
        [
            jnp.broadcast_to(ref[h : h + 1, :], (images, width))
            for ref in (q0, q1)
            for h in range(heads)
        ],
        0,
    )
    columns = spread.shape[0]
    high = spread.astype(BF16)
    low = (spread - high.astype(F32)).astype(BF16)
    both = jnp.concatenate([high, low], 0)
    sides, raw = [], []
    for i, copy in enumerate(copies):
        copy.wait()
        sides.append(near_ref[i].reshape(images * here, width))
        raw.append(lax.dot_general(both, sides[i], NT, preferred_element_type=F32))
    raw = jnp.concatenate(raw, 1)
    scores = raw[:columns] + raw[columns:]
    row_image = lax.broadcasted_iota(jnp.int32, scores.shape, 0) % images
    token_image = lax.broadcasted_iota(jnp.int32, scores.shape, 1) // here % images
    mine = row_image == token_image
    top = jnp.max(jnp.where(mine, scores, -jnp.inf), 1, keepdims=True)
    raised = jnp.exp(jnp.where(mine, scores - top, -jnp.inf))
    total = jnp.sum(raised, 1, keepdims=True)
    weights = (raised / total).astype(BF16)
    split = images * here
    mixed = jnp.dot(weights[:, :split], sides[0], preferred_element_type=F32)
    mixed = mixed + jnp.dot(weights[:, split:], sides[1], preferred_element_type=F32)
    mixed = mixed.astype(BF16)
    log_total = top + jnp.log(total)
    high = log_total.astype(BF16).astype(F32)
    middle = (log_total - high).astype(BF16).astype(F32)
    low = log_total - high - middle
    lane = lax.broadcasted_iota(jnp.int32, (columns, 128), 1)
    pieces = jnp.where(lane == 0, high, jnp.where(lane == 1, middle, jnp.where(lane == 2, low, 0.0)))
    pieces = pieces.astype(BF16)
    step = columns // 2
    for s, ref in enumerate((m0, m1)):
        ref[:, :width] = mixed[s * step : (s + 1) * step]
        ref[:, width:] = pieces[s * step : (s + 1) * step]


def embed_kernel(m0, m1, value_ref, final_ref, out_ref, *, heads):
    width = value_ref.shape[0]
    parts = (m0, m1)
    logs = [jnp.sum(ref[:, width:].astype(F32), -1, keepdims=True) for ref in parts]
    peak = jnp.maximum(logs[0], logs[1])
    shares = [jnp.exp(entry - peak) for entry in logs]
    whole = shares[0] + shares[1]
    mixed = sum((s / whole) * ref[:, :width].astype(F32) for s, ref in zip(shares, parts))
    pooled = jnp.dot(mixed.astype(BF16), value_ref[...], preferred_element_type=F32)
    rows, columns = pooled.shape
    images = rows // heads
    row_head = lax.broadcasted_iota(jnp.int32, pooled.shape, 0) // images
    column_head = lax.broadcasted_iota(jnp.int32, pooled.shape, 1) // (columns // heads)
    kept = jnp.where(row_head == column_head, pooled, 0.0)
    pooled = sum(kept[h * images : (h + 1) * images] for h in range(heads))
    out_ref[...] = jnp.dot(pooled.astype(BF16), final_ref[...], preferred_element_type=F32)


def unit_kernel(e0, e1, e2, e3, order1, order2, order3, unit_ref):
    embed = (e0[...] + e1[...]) + (e2[...] + e3[...])
    unit_ref[...] = unit_rows(embed)


def text_grad_kernel(place_ref, scalar_ref, u0, u1, u2, u3, text_ref, order_ref, part_ref, *, near):
    dp, head = place_ref[0], place_ref[1]
    multiplier, shift = scalar_ref[0], scalar_ref[1]
    images, width = u0.shape
    chunk = width // 4
    block = dp // near
    units = jnp.concatenate([ref[...].astype(F32) for ref in (u0, u1, u2, u3)], 0)
    logits = halves_product(units.astype(BF16), text_ref[...]) * multiplier + shift
    row = lax.broadcasted_iota(jnp.int32, logits.shape, 0)
    image_id = ((block ^ (row // images)) * near + dp % near) * images + row % images
    text_id = text_ids(logits.shape, block * near, images, head)
    matched = jnp.where(image_id == text_id, 1.0, 0.0)
    coefficient = (multiplier * (jax.nn.sigmoid(logits) - matched)).astype(BF16)
    source = lax.broadcasted_iota(jnp.int32, (near * 8, near * 8), 0)
    target = lax.broadcasted_iota(jnp.int32, (near * 8, near * 8), 1)
    repeat = jnp.where(source == target // 8 * 8 + head // 2 * 2 + target % 8 // 4, 1.0, 0.0)
    wide = jnp.dot(coefficient, repeat.astype(BF16), preferred_element_type=F32)
    wide = jnp.concatenate([wide] * 4, 0)
    row_chunk = lax.broadcasted_iota(jnp.int32, wide.shape, 0) // (4 * images)
    column_chunk = lax.broadcasted_iota(jnp.int32, wide.shape, 1) % 4
    wide = jnp.where(row_chunk == column_chunk, wide, 0.0).astype(BF16)
    stacked = jnp.concatenate([units[:, c * chunk : (c + 1) * chunk] for c in range(4)], 0)
    part = lax.dot_general(wide, stacked.astype(BF16), TN, preferred_element_type=F32)
    part_ref[...] = part.reshape(part_ref.shape).astype(part_ref.dtype)


def image_grad_kernel(
    place_ref, scalar_ref, unit_ref, t0, t1, t2, t3, own_ref, other_ref, *, near
):
    dp, head = place_ref[0], place_ref[1]
    multiplier, shift = scalar_ref[0], scalar_ref[1]
    images, width = unit_ref.shape
    share = images // 4
    block = dp // near
    texts = [ref[...] for ref in (t0, t1, t2, t3)]
    count = texts[0].shape[0]
    logits = jnp.concatenate([halves_product(unit_ref[...], part) for part in texts], 1)
    logits = logits * multiplier + shift
    image_id = dp * images + lax.broadcasted_iota(jnp.int32, logits.shape, 0)
    column = lax.broadcasted_iota(jnp.int32, logits.shape, 1)
    first_dp = ((column // count) ^ block) * near
    text_id = (first_dp + column % count // 8 * 7 % near) * images
    text_id = text_id + column % 4 // 2 * 4 + head % 2 * 2 + column % 2
    matched = jnp.where(image_id == text_id, 1.0, 0.0)
    coefficient = multiplier * (jax.nn.sigmoid(logits) - matched)
    upper = column % 8 // 4 == 1
    sides = jnp.concatenate(
        [jnp.where(upper, 0.0, coefficient), jnp.where(upper, coefficient, 0.0)], 0
    ).astype(BF16)
    grads = sum(
        jnp.dot(sides[:, s * count : (s + 1) * count], part, preferred_element_type=F32)
        for s, part in enumerate(texts)
    )
    grads = jnp.concatenate([grads[:images], grads[images:]], 1)
    for wanted, ref in ((head, own_ref), (head ^ 1, other_ref)):
        ref[...] = sum(
            jnp.where(wanted == k, grads[k * share : (k + 1) * share], 0.0) for k in range(4)
        )


def sum_kernel(part_ref, own_ref, other_ref, image_ref, out_ref):
    image_ref[...] = own_ref[...] + other_ref[...]
    share, width = out_ref.shape
    chunk = part_ref.shape[2]
    total = jnp.sum(part_ref[...].astype(F32), 0)
    for r in range(share):
        for c in range(4):
            out_ref[r : r + 1, c * chunk : (c + 1) * chunk] = total[r * 4 + c : r * 4 + c + 1]


def per_device(tokens, projector, queries, final, captions, multiplier, shift):
    images, here, width = tokens.shape
    heads, head_size = queries.shape
    n_dp = lax.axis_size("dp")
    near = n_dp // 4
    share = images // 4
    dp = lax.axis_index("dp")
    head = lax.axis_index("head")
    columns = heads * head_size

    both = projector.reshape(width, 2 * columns)
    own = (jnp.arange(columns) // head_size)[None, :] == jnp.arange(heads)[:, None]
    spread = jnp.where(own, jnp.tile(queries, (1, heads)), 0).astype(BF16)
    key_spec = pl.BlockSpec((width, columns), lambda i: (0, 0), memory_space=pltpu.VMEM)
    value_spec = pl.BlockSpec((width, columns), lambda i: (0, 1), memory_space=pltpu.VMEM)

    def f32(*shape):
        return jax.ShapeDtypeStruct(shape, F32)

    def bf16(*shape):
        return jax.ShapeDtypeStruct(shape, BF16)

    other_tokens = peer(tokens, 1)
    place = jnp.stack([dp, head]).astype(jnp.int32)
    key_query, text_copies = call(
        lambda *refs: first_kernel(*refs, scale=1.0 / math.sqrt(head_size)),
        [f32(heads, width), bf16(near, images, width // 2)],
        [SMEM, VMEM, key_spec, VMEM],
        2 * heads * width * columns,
        2 * width * columns,
        [pltpu.VMEM((near, images, width // 2), BF16), pltpu.SemaphoreType.DMA],
        out_specs=[VMEM, ANY],
    )(place, spread, both, captions)

    groups = [[b * near + i * 7 % near for i in range(near)] for b in range(4)]

    def swap(pieces):
        return lax.all_to_all(pieces, "dp", 0, 0, axis_index_groups=groups, tiled=False)

    def across(pieces):
        return [pieces[0]] + [
            lax.ppermute(pieces[s], "dp", [(i, i ^ (s * near)) for i in range(n_dp)])
            for s in (1, 2, 3)
        ]

    texts = swap(text_copies).reshape(near * images, width // 2)
    all_texts = across([texts] * 4)

    mixes = call(
        lambda *refs: mix_kernel(*refs, images=images),
        [bf16(heads * images, width + 128)] * 2,
        [ANY, ANY, VMEM, VMEM],
        64 << 30,
        6 * images * here * width,
        [pltpu.VMEM((2, *tokens.shape), BF16), pltpu.SemaphoreType.DMA((2,))],
        53,
    )(tokens, other_tokens, key_query, peer(key_query, 2))
    embeds = call(
        lambda *refs: embed_kernel(*refs, heads=heads),
        f32(images, width),
        [VMEM, VMEM, value_spec, VMEM],
        64 << 30,
        4 * width * columns,
    )(mixes[0], peer(mixes[1], 2), both, final)
    embeds = [embeds] + [peer(embeds, s) for s in (1, 2, 3)]

    scalars = jnp.stack([multiplier, shift])
    unit = call(
        unit_kernel,
        bf16(images, width),
        [VMEM] * 4 + [ANY] * 3,
        8 * images * width,
        18 * images * width,
    )(*embeds, *all_texts[1:])
    units = across([unit] * 4)
    own_part, other_part = call(
        lambda *refs: image_grad_kernel(*refs, near=near),
        [f32(share, width)] * 2,
        [SMEM, SMEM] + [VMEM] * 5,
        2 * 64 * n_dp * width,
        16 * n_dp * width,
    )(place, scalars, unit, *all_texts)
    other_part = peer(other_part, 1)
    text_part = call(
        lambda *refs: text_grad_kernel(*refs, near=near),
        bf16(near, 4 * share, width // 4),
        [SMEM, SMEM] + [VMEM] * 5 + [ANY],
        2 * 256 * near * width,
        8 * near * width,
    )(place, scalars, *units, texts, other_part)
    received = swap(text_part)
    image_grad, text_grad = call(
        sum_kernel, [f32(share, width)] * 2, [VMEM] * 3, near * share * width, 2 * near * share * width
    )(received, own_part, other_part)
    return image_grad, text_grad


def solution(mesh):
    in_specs = (
        P("dp", "head", None),
        P(None, None, "head"),
        P("head", None),
        P("head", None),
        P("dp", None),
        P(),
        P(),
    )
    out_specs = (P(("dp", "head"), None), P(("dp", "head"), None))
    return jax.shard_map(
        per_device, mesh=mesh, in_specs=in_specs, out_specs=out_specs, check_vma=False
    )
```

```python
import math

import jax
import jax.numpy as jnp
from jax import lax
from jax.experimental import pallas as pl
from jax.experimental.pallas import tpu as pltpu
from jax.sharding import PartitionSpec as P

F32 = jnp.float32
BF16 = jnp.bfloat16
NT = (((1,), (1,)), ((), ()))
TN = (((0,), (0,)), ((), ()))
VMEM = pl.BlockSpec(memory_space=pltpu.VMEM)
ANY = pl.BlockSpec(memory_space=pl.ANY)
HBM = pl.BlockSpec(memory_space=pltpu.HBM)
SMEM = pl.BlockSpec(memory_space=pltpu.SMEM)


def call(kernel, outs, specs, flops, moved, scratch=(), limit=12):
    return pl.pallas_call(
        kernel,
        grid=(1,),
        out_shape=outs,
        in_specs=specs,
        out_specs=jax.tree.map(lambda _: VMEM, outs),
        scratch_shapes=scratch,
        compiler_params=pltpu.CompilerParams(vmem_limit_bytes=limit << 20),
        cost_estimate=pl.CostEstimate(flops=flops, bytes_accessed=moved, transcendentals=0),
    )


def unit_rows(values):
    widened = values.astype(F32)
    return (widened * lax.rsqrt(jnp.sum(widened * widened, -1, keepdims=True) + 1e-06)).astype(BF16)


def peer(piece, step):
    return lax.ppermute(piece, "head", [(i, i ^ step) for i in range(4)])


def key_query_kernel(spread_ref, key_ref, out_ref, *, scale):
    out_ref[...] = (
        lax.dot_general(spread_ref[...], key_ref[...], NT, preferred_element_type=F32) * scale
    )


def mix_kernel(own_ref, other_ref, q0, q1, m0, m1, near_ref, done, *, images):
    copies = [
        pltpu.make_async_copy(ref, near_ref.at[i], done.at[i])
        for i, ref in enumerate((own_ref, other_ref))
    ]
    for copy in copies:
        copy.start()
    here, width = own_ref.shape[1:]
    heads = q0.shape[0]
    spread = jnp.concatenate(
        [
            jnp.broadcast_to(ref[h : h + 1, :], (images, width))
            for ref in (q0, q1)
            for h in range(heads)
        ],
        0,
    )
    columns = spread.shape[0]
    high = spread.astype(BF16)
    low = (spread - high.astype(F32)).astype(BF16)
    both = jnp.concatenate([high, low], 0)
    sides, raw = [], []
    for i, copy in enumerate(copies):
        copy.wait()
        sides.append(near_ref[i].reshape(images * here, width))
        raw.append(lax.dot_general(both, sides[i], NT, preferred_element_type=F32))
    raw = jnp.concatenate(raw, 1)
    scores = raw[:columns] + raw[columns:]
    row_image = lax.broadcasted_iota(jnp.int32, scores.shape, 0) % images
    token_image = lax.broadcasted_iota(jnp.int32, scores.shape, 1) // here % images
    mine = row_image == token_image
    top = jnp.max(jnp.where(mine, scores, -jnp.inf), 1, keepdims=True)
    raised = jnp.exp(jnp.where(mine, scores - top, -jnp.inf))
    total = jnp.sum(raised, 1, keepdims=True)
    weights = (raised / total).astype(BF16)
    split = images * here
    mixed = jnp.dot(weights[:, :split], sides[0], preferred_element_type=F32)
    mixed = mixed + jnp.dot(weights[:, split:], sides[1], preferred_element_type=F32)
    mixed = mixed.astype(BF16)
    log_total = top + jnp.log(total)
    high = log_total.astype(BF16).astype(F32)
    middle = (log_total - high).astype(BF16).astype(F32)
    low = log_total - high - middle
    lane = lax.broadcasted_iota(jnp.int32, (columns, 128), 1)
    pieces = jnp.where(lane == 0, high, jnp.where(lane == 1, middle, jnp.where(lane == 2, low, 0.0)))
    pieces = pieces.astype(BF16)
    step = columns // 2
    for s, ref in enumerate((m0, m1)):
        ref[:, :width] = mixed[s * step : (s + 1) * step]
        ref[:, width:] = pieces[s * step : (s + 1) * step]


def embed_kernel(m0, m1, value_ref, final_ref, out_ref, short_ref, near_ref, done, *, heads):
    copy = pltpu.make_async_copy(final_ref, near_ref, done)
    copy.start()
    width = value_ref.shape[0]
    parts = (m0, m1)
    logs = [jnp.sum(ref[:, width:].astype(F32), -1, keepdims=True) for ref in parts]
    peak = jnp.maximum(logs[0], logs[1])
    shares = [jnp.exp(entry - peak) for entry in logs]
    whole = shares[0] + shares[1]
    mixed = sum((s / whole) * ref[:, :width].astype(F32) for s, ref in zip(shares, parts))
    pooled = jnp.dot(mixed.astype(BF16), value_ref[...], preferred_element_type=F32)
    rows, columns = pooled.shape
    images = rows // heads
    row_head = lax.broadcasted_iota(jnp.int32, pooled.shape, 0) // images
    column_head = lax.broadcasted_iota(jnp.int32, pooled.shape, 1) // (columns // heads)
    kept = jnp.where(row_head == column_head, pooled, 0.0)
    pooled = sum(kept[h * images : (h + 1) * images] for h in range(heads))
    copy.wait()
    embed = jnp.dot(pooled.astype(BF16), near_ref[...], preferred_element_type=F32)
    out_ref[...] = embed
    short_ref[...] = embed.astype(BF16)


def text_kernel(place_ref, captions_ref, order_ref, out_ref):
    core = place_ref[1] % 2
    unit = unit_rows(captions_ref[...]).astype(F32)
    first = jnp.concatenate([unit[0:2], unit[4:6]], 0)
    second = jnp.concatenate([unit[2:4], unit[6:8]], 0)
    chosen = jnp.where(core == 0, first, second).astype(BF16)
    out_ref[...] = jnp.broadcast_to(chosen[None], out_ref.shape)


def rows_kernel(text_ref, order_ref, rows_ref):
    texts = text_ref[...].astype(F32)
    rows_ref[...] = jnp.concatenate([texts[i] for i in range(texts.shape[0])], 0).astype(BF16)


def text_ids(shape, first_dp, images, head):
    column = lax.broadcasted_iota(jnp.int32, shape, 1)
    return (first_dp + column // 4) * images + column % 4 // 2 * 4 + head % 2 * 2 + column % 2


def unit_kernel(e0, e1, e2, e3, order1, order2, order3, unit_ref):
    parts = [ref[...].astype(F32) for ref in (e0, e1, e2, e3)]
    embed = (parts[0] + parts[1]) + (parts[2] + parts[3])
    unit_ref[...] = unit_rows(embed)


def text_grad_kernel(place_ref, scalar_ref, u0, u1, u2, u3, text_ref, order_ref, part_ref, *, near):
    dp, head = place_ref[0], place_ref[1]
    multiplier, shift = scalar_ref[0], scalar_ref[1]
    images, width = u0.shape
    chunk = width // 4
    block = dp // near
    units = jnp.concatenate([ref[...].astype(F32) for ref in (u0, u1, u2, u3)], 0)
    logits = lax.dot_general(units.astype(BF16), text_ref[...], NT, preferred_element_type=F32)
    logits = logits * multiplier + shift
    row = lax.broadcasted_iota(jnp.int32, logits.shape, 0)
    image_id = ((block ^ (row // images)) * near + dp % near) * images + row % images
    text_id = text_ids(logits.shape, block * near, images, head)
    matched = jnp.where(image_id == text_id, 1.0, 0.0)
    coefficient = (multiplier * (jax.nn.sigmoid(logits) - matched)).astype(BF16)
    source = lax.broadcasted_iota(jnp.int32, (near * 4, near * 8), 0)
    target = lax.broadcasted_iota(jnp.int32, (near * 4, near * 8), 1)
    repeat = jnp.where(source == target // 8 * 4 + head // 2 * 2 + target % 8 // 4, 1.0, 0.0)
    wide = jnp.dot(coefficient, repeat.astype(BF16), preferred_element_type=F32)
    wide = jnp.concatenate([wide] * 4, 0)
    row_chunk = lax.broadcasted_iota(jnp.int32, wide.shape, 0) // (4 * images)
    column_chunk = lax.broadcasted_iota(jnp.int32, wide.shape, 1) % 4
    wide = jnp.where(row_chunk == column_chunk, wide, 0.0).astype(BF16)
    stacked = jnp.concatenate([units[:, c * chunk : (c + 1) * chunk] for c in range(4)], 0)
    part = lax.dot_general(wide, stacked.astype(BF16), TN, preferred_element_type=F32)
    part_ref[...] = part.reshape(part_ref.shape).astype(part_ref.dtype)


def image_grad_kernel(
    place_ref, scalar_ref, unit_ref, t0, t1, t2, t3, own_ref, other_ref, *, near
):
    dp, head = place_ref[0], place_ref[1]
    multiplier, shift = scalar_ref[0], scalar_ref[1]
    images, width = unit_ref.shape
    share = images // 4
    block = dp // near
    texts = [ref[...] for ref in (t0, t1, t2, t3)]
    count = texts[0].shape[0]
    logits = [
        lax.dot_general(unit_ref[...], part, NT, preferred_element_type=F32) for part in texts
    ]
    logits = jnp.concatenate(logits, 1) * multiplier + shift
    image_id = dp * images + lax.broadcasted_iota(jnp.int32, logits.shape, 0)
    column = lax.broadcasted_iota(jnp.int32, logits.shape, 1)
    first_dp = ((column // count) ^ block) * near
    text_id = (first_dp + column % count // 4) * images
    text_id = text_id + column % 4 // 2 * 4 + head % 2 * 2 + column % 2
    matched = jnp.where(image_id == text_id, 1.0, 0.0)
    coefficient = (multiplier * (jax.nn.sigmoid(logits) - matched)).astype(BF16)
    grads = sum(
        jnp.dot(coefficient[:, s * count : (s + 1) * count], part, preferred_element_type=F32)
        for s, part in enumerate(texts)
    )
    for wanted, ref in ((head, own_ref), (head ^ 1, other_ref)):
        ref[...] = sum(
            jnp.where(wanted == k, grads[k * share : (k + 1) * share], 0.0) for k in range(4)
        )


def sum_kernel(part_ref, own_ref, other_ref, image_ref, out_ref):
    image_ref[...] = own_ref[...] + other_ref[...]
    share, width = out_ref.shape
    chunk = part_ref.shape[2]
    total = jnp.sum(part_ref[...].astype(F32), 0)
    for r in range(share):
        for c in range(4):
            out_ref[r : r + 1, c * chunk : (c + 1) * chunk] = total[r * 4 + c : r * 4 + c + 1]


def per_device(tokens, projector, queries, final, captions, multiplier, shift):
    images, here, width = tokens.shape
    heads, head_size = queries.shape
    n_dp = lax.axis_size("dp")
    near = n_dp // 4
    share = images // 4
    dp = lax.axis_index("dp")
    head = lax.axis_index("head")
    columns = heads * head_size

    both = projector.reshape(width, 2 * columns)
    own = (jnp.arange(columns) // head_size)[None, :] == jnp.arange(heads)[:, None]
    spread = jnp.where(own, jnp.tile(queries, (1, heads)), 0).astype(BF16)
    key_spec = pl.BlockSpec((width, columns), lambda i: (0, 0), memory_space=pltpu.VMEM)
    value_spec = pl.BlockSpec((width, columns), lambda i: (0, 1), memory_space=pltpu.VMEM)

    def f32(*shape):
        return jax.ShapeDtypeStruct(shape, F32)

    def bf16(*shape):
        return jax.ShapeDtypeStruct(shape, BF16)

    other_tokens = peer(tokens, 1)
    key_query = call(
        lambda *refs: key_query_kernel(*refs, scale=1.0 / math.sqrt(head_size)),
        f32(heads, width),
        [VMEM, key_spec],
        2 * heads * width * columns,
        2 * width * columns,
    )(spread, both)

    place = jnp.stack([dp, head]).astype(jnp.int32)
    groups = [[b * near + i for i in range(near)] for b in range(4)]

    def swap(pieces):
        return lax.all_to_all(pieces, "dp", 0, 0, axis_index_groups=groups, tiled=False)

    def across(pieces):
        return [pieces[0]] + [
            lax.ppermute(pieces[s], "dp", [(i, i ^ (s * near)) for i in range(n_dp)])
            for s in (1, 2, 3)
        ]

    text_copies = call(
        text_kernel, bf16(near, 4, width), [SMEM, VMEM, ANY], 6 << 30, 8 * n_dp * width
    )(place, captions, key_query)
    copies = swap(text_copies)

    mixes = call(
        lambda *refs: mix_kernel(*refs, images=images),
        [bf16(heads * images, width + 128)] * 2,
        [ANY, ANY, VMEM, VMEM],
        64 << 30,
        6 * images * here * width,
        [pltpu.VMEM((2, *tokens.shape), BF16), pltpu.SemaphoreType.DMA((2,))],
        53,
    )(tokens, other_tokens, key_query, peer(key_query, 2))
    texts = call(
        rows_kernel, bf16(near * 4, width), [VMEM, ANY], near * 4 * width, 16 * near * width
    )(copies, mixes[0])
    all_texts = across([texts] * 4)
    embeds, short_embeds = call(
        lambda *refs: embed_kernel(*refs, heads=heads),
        [f32(images, width), bf16(images, width)],
        [VMEM, VMEM, value_spec, ANY],
        64 << 30,
        4 * width * columns,
        [pltpu.VMEM(final.shape, BF16), pltpu.SemaphoreType.DMA],
        52,
    )(mixes[0], peer(mixes[1], 2), both, final)
    embeds = [embeds] + [peer(short_embeds, s) for s in (1, 2, 3)]

    scalars = jnp.stack([multiplier, shift])
    unit = call(
        unit_kernel,
        bf16(images, width),
        [VMEM] * 4 + [ANY] * 3,
        8 * images * width,
        18 * images * width,
    )(*embeds, *all_texts[1:])
    units = across([unit] * 4)
    own_part, other_part = call(
        lambda *refs: image_grad_kernel(*refs, near=near),
        [f32(share, width)] * 2,
        [SMEM, SMEM] + [VMEM] * 5,
        2 * 64 * n_dp * width,
        16 * n_dp * width,
    )(place, scalars, unit, *all_texts)
    other_part = peer(other_part, 1)
    text_part = call(
        lambda *refs: text_grad_kernel(*refs, near=near),
        bf16(near, 4 * share, width // 4),
        [SMEM, SMEM] + [VMEM] * 5 + [ANY],
        2 * 256 * near * width,
        8 * near * width,
    )(place, scalars, *units, texts, other_part)
    received = swap(text_part)
    image_grad, text_grad = call(
        sum_kernel, [f32(share, width)] * 2, [VMEM] * 3, near * share * width, 2 * near * share * width
    )(received, own_part, other_part)
    return image_grad, text_grad


def solution(mesh):
    in_specs = (
        P("dp", "head", None),
        P(None, None, "head"),
        P("head", None),
        P("head", None),
        P("dp", None),
        P(),
        P(),
    )
    out_specs = (P(("dp", "head"), None), P(("dp", "head"), None))
    return jax.shard_map(
        per_device, mesh=mesh, in_specs=in_specs, out_specs=out_specs, check_vma=False
    )
```
